128 devices in a mesh: blk: 64 (over y, x_lo, z, core), tower: 2 (over x_hi).
Axes of the slice: x: 4 (x_hi: 2, x_lo: 2; x = x_hi * 2 + x_lo), y: 4, z: 4, core: 2. Of those that a mesh axis runs over, the one named last changes fastest.
Arguments:
- vision_features: bfloat16 [65536, 1152], P('blk', 'tower'), may hold values from -36 to 36
- caption_features: bfloat16 [65536, 1152], P('blk', 'tower'), may hold values from -36 to 36
- sample_importance: bfloat16 [65536], P('blk'), may hold values from 0.5 to 18, as said below
- scale_exponent: float32 [1], replicated, may hold values from 2.3 to 3.4
- similarity_shift: float32 [1], replicated, may hold values from -3 to -1
Outputs:
- image_gradient: bfloat16 [65536, 1152], P('blk', 'tower')
- text_gradient: bfloat16 [65536, 1152], P('blk', 'tower')
- scalars: float32 [3], replicated
The draws below stay inside these ranges and needn't reach their ends.
Inputs may be any that keep to these rules, and one draw needn't show every extreme that they name: `sample_importance`: positive loss weight of each pair.
All inputs are finite; a program needn't handle non-finite values.
Results may differ from the reference program's by a relative error of at most 0.012.
Values may be sent and summed in bfloat16 or wider, within the bound.
A program may use at most 64 MiB of HBM per device.

```python
import math
import jax
import jax.numpy as jnp
from jax import lax

FEATURE_SPAN = 1152
ROWS = 512
HALF = 2
EXAMPLE_COUNT = 65536
BAND = 2560


def scaled_field(key, row_count, col_count):
    subkeys = jax.random.split(key, 3)
    col_scale = jnp.exp(jax.random.uniform(subkeys[0], (1, col_count), jnp.float32, math.log(0.3), math.log(3.0)))
    row_scale = jnp.exp(jax.random.uniform(subkeys[1], (row_count, 1), jnp.float32, math.log(0.3), math.log(3.0)))
    gaussian = jnp.clip(jax.random.normal(subkeys[2], (row_count, col_count), jnp.float32), -4.0, 4.0)
    noise_field = gaussian
    return noise_field * col_scale * row_scale


def draw_vision_features(key, part):
    key = jax.random.fold_in(key, 11)
    return scaled_field(key, EXAMPLE_COUNT, FEATURE_SPAN).astype(jnp.bfloat16)


def draw_caption_features(key, part):
    key = jax.random.fold_in(key, 17)
    return scaled_field(key, EXAMPLE_COUNT, FEATURE_SPAN).astype(jnp.bfloat16)


def draw_sample_importance(key, part):
    key = jax.random.fold_in(key, 23)
    position = jnp.arange(EXAMPLE_COUNT, dtype=jnp.float32) / float(EXAMPLE_COUNT - 1)
    return (jnp.exp(math.log(3.0) * position) * jnp.exp(jax.random.uniform(key, (EXAMPLE_COUNT,), jnp.float32, math.log(0.5), math.log(2.0)))).astype(jnp.bfloat16)


def setup_inputs(seed: int = 0) -> dict:
    streams_of = jax.random.split(jax.random.key(seed), 6)
    return {
        "vision_features": draw_vision_features(jax.random.fold_in(streams_of[5], 71), 0),
        "caption_features": draw_caption_features(jax.random.fold_in(streams_of[5], 71), 0),
        "sample_importance": draw_sample_importance(jax.random.fold_in(streams_of[5], 71), 0),
        "scale_exponent": jnp.clip(jax.random.uniform(streams_of[3], (1,), jnp.float32, 2.3, 3.4), 2.3, 3.4),
        "similarity_shift": jnp.clip(jax.random.uniform(streams_of[4], (1,), jnp.float32, -3.0, -1.0), -3.0, -1.0),
    }


def unit_rows(values):
    wide = values.astype(jnp.float32)
    row_norm = jnp.sqrt(lax.optimization_barrier(jnp.sum(wide * wide, axis=1, keepdims=True)) + 1e-06)
    return (wide / row_norm, row_norm)

def norm_gradient_backward(unit_wide, row_norm, direction):
    along = lax.optimization_barrier(jnp.sum(unit_wide * direction, axis=1, keepdims=True))
    return ((direction - unit_wide * along) / row_norm).astype(jnp.bfloat16)

def reference(vision_features, caption_features, sample_importance, scale_exponent, similarity_shift):
    picture_full_vectors, picture_length = unit_rows(vision_features)
    caption_full_vectors, caption_length = unit_rows(caption_features)
    image_unit_rows = picture_full_vectors.astype(jnp.bfloat16)
    txt_unit = caption_full_vectors.astype(jnp.bfloat16)
    similarity_scale = jnp.exp(scale_exponent[0])
    logit_bias_value = similarity_shift[0]
    weights = sample_importance.astype(jnp.float32)
    blocks = EXAMPLE_COUNT // ROWS
    diagonal_mask = (jnp.arange(ROWS)[:, None] == jnp.arange(ROWS)[None, :]).astype(jnp.float32)

    def one_block(carried, block_index):
        caption_running_sum, tallies = carried
        img_start = (block_index * ROWS).astype(jnp.int32)
        image_block = lax.dynamic_slice_in_dim(image_unit_rows, img_start, ROWS, 0)
        row_weight_factor = lax.dynamic_slice_in_dim(weights, img_start, ROWS, 0)[:, None]
        picture_running_sum = jnp.zeros((ROWS, FEATURE_SPAN), jnp.float32)
        for block_offset in range(-HALF, HALF + 1):
            txt_start = ((block_index + block_offset) % blocks * ROWS).astype(jnp.int32)
            text_block = lax.dynamic_slice_in_dim(txt_unit, txt_start, ROWS, 0)
            cosine_matrix = jnp.dot(image_block, text_block.T, preferred_element_type=jnp.float32)
            scaled_similarity = similarity_scale * cosine_matrix
            logits = scaled_similarity + logit_bias_value
            if block_offset == 0:
                losses = jax.nn.softplus(logits) - diagonal_mask * logits
                coef_wide = row_weight_factor * (jax.nn.sigmoid(logits) - diagonal_mask)
            else:
                losses = jax.nn.softplus(logits)
                coef_wide = row_weight_factor * jax.nn.sigmoid(logits)
            coef_half = coef_wide.astype(jnp.bfloat16)
            picture_running_sum = picture_running_sum + jnp.dot(coef_half, text_block, preferred_element_type=jnp.float32)
            txt_term = jnp.dot(coef_half.T, image_block, preferred_element_type=jnp.float32)
            current = lax.dynamic_slice_in_dim(caption_running_sum, txt_start, ROWS, 0)
            caption_running_sum = lax.dynamic_update_slice_in_dim(caption_running_sum, current + txt_term, txt_start, 0)
            tallies = tallies + jnp.stack([jnp.sum(row_weight_factor * losses), jnp.sum(coef_wide * scaled_similarity), jnp.sum(coef_wide)])
        return ((caption_running_sum, tallies), picture_running_sum)
    start_state = (jnp.zeros((EXAMPLE_COUNT, FEATURE_SPAN), jnp.float32), jnp.zeros((3,), jnp.float32))
    (caption_running_sum, tallies), picture_running_sums = lax.scan(one_block, start_state, jnp.arange(blocks, dtype=jnp.int32))
    picture_normalized = similarity_scale * picture_running_sums.reshape(EXAMPLE_COUNT, FEATURE_SPAN)
    caption_normalized = similarity_scale * caption_running_sum
    image_gradient = norm_gradient_backward(picture_full_vectors, picture_length, picture_normalized)
    text_gradient = norm_gradient_backward(caption_full_vectors, caption_length, caption_normalized)
    scalars = tallies / jnp.float32(EXAMPLE_COUNT * BAND)
    return (image_gradient, text_gradient, scalars)
```

```python
import functools
import math

import jax
import jax.numpy as jnp
from jax import lax
from jax.experimental import pallas as pl
from jax.experimental.pallas import tpu as pltpu
from jax.sharding import PartitionSpec as P

MESH = pl.DeviceIdType.MESH
F32, BF16 = jnp.float32, jnp.bfloat16
TXT, IMG = 0, 1
BLOCK = 512
SUPER = 1024
PART = 576
FULL = 1152
CHUNK = 256
CHUNKS = SUPER // CHUNK
LINE = 8
LOG2E = math.log2(math.e)


def fold(v):
    total = v[:, :128]
    for k in range(1, v.shape[1] // 128):
        total = total + v[:, 128 * k : 128 * (k + 1)]
    return total


def row_of(partial):
    return jnp.sum(jnp.transpose(partial), axis=0, keepdims=True)


def kernel(
    count,
    txt_in,
    img_in,
    weight_in,
    exponent,
    offset,
    img_out,
    txt_out,
    sums_out,
    held,
    weights,
    inv_row,
    inv_col,
    turned_txt,
    turned_img,
    txt_grad,
    txt_along,
    tallies,
    staged,
    coef,
    line_sums,
    all_sums,
    load_sem,
    x_send,
    x_recv,
    own_send,
    own_recv,
    other_send,
    other_recv,
    weight_send,
    weight_recv,
    out_sem,
    line_send,
    line_recv,
    all_send,
    all_recv,
):
    sb = lax.axis_index("blk")
    tower = lax.axis_index("tower")
    away = 1 - tower
    left, right = lax.rem(sb + count - 1, count), lax.rem(sb + 1, count)
    place, line = lax.rem(sb, LINE), sb // LINE
    lines = count // LINE
    rank = place * 2 + tower
    left_end, right_end = place == 0, place == LINE - 1
    inputs = (txt_in, img_in)
    sides = ((0, left, left_end), (1, right, right_end))

    def line_peer(k):
        there = lax.rem(rank + k, 2 * LINE)
        return there, (line * LINE + there // 2, lax.rem(there, 2))

    def all_peer(k):
        there = lax.rem(line + k, lines)
        return there, (there * LINE + place, tower)

    def columns_of(slot, c):
        return pl.ds(pl.multiple_of(slot * SUPER + c * CHUNK, CHUNK), CHUNK)

    def whole(slot):
        return pl.ds(slot * SUPER, SUPER)

    loads = []
    for a in range(2):
        target = held.at[a, pl.ds(0, PART), whole(1)]
        loads.append(pltpu.make_async_copy(inputs[a], target, load_sem.at[a]))
        loads[a].start()

    barrier = pltpu.get_barrier_semaphore()

    def greet(where):
        pl.semaphore_signal(barrier, inc=1, device_id=where, device_id_type=MESH)

    for where in ((sb, away), (left, tower), (right, tower)):
        greet(where)

    @pl.when(left_end)
    def _():
        greet((left, away))

    @pl.when(right_end)
    def _():
        greet((right, away))

    def greet_line(k, carry):
        greet(line_peer(k)[1])
        return carry

    def greet_all(k, carry):
        greet(all_peer(k)[1])
        return carry

    lax.fori_loop(1, 2 * LINE, greet_line, 0)
    lax.fori_loop(1, lines, greet_all, 0)
    at_end = jnp.logical_or(left_end, right_end)
    pl.semaphore_wait(barrier, jnp.where(at_end, 4, 3) + (2 * LINE - 1) + (lines - 1))

    def x_copy(a, c):
        return pltpu.make_async_remote_copy(
            src_ref=inputs[a].at[:, pl.ds(c * CHUNK, CHUNK)],
            dst_ref=held.at[a, pl.ds(PART, PART), columns_of(1, c)],
            send_sem=x_send.at[a, c],
            recv_sem=x_recv.at[a, c],
            device_id=(sb, away),
            device_id_type=MESH,
        )

    def own_copy(a, side):
        n, where, _ = sides[side]
        return pltpu.make_async_remote_copy(
            src_ref=inputs[a],
            dst_ref=held.at[a, pl.ds(0, PART), whole(2 - 2 * n)],
            send_sem=own_send.at[a, n],
            recv_sem=own_recv.at[a, n],
            device_id=(where, tower),
            device_id_type=MESH,
        )

    def other_copy(a, side, c):
        n, where, end = sides[side]
        first = pl.multiple_of(jnp.where(end, 0, PART), 64)
        return pltpu.make_async_remote_copy(
            src_ref=held.at[a, pl.ds(first, PART), columns_of(1, c)],
            dst_ref=held.at[a, pl.ds(PART, PART), columns_of(2 - 2 * n, c)],
            send_sem=other_send.at[a, n, c],
            recv_sem=other_recv.at[a, n, c],
            device_id=(where, jnp.where(end, away, tower)),
            device_id_type=MESH,
        )

    def weight_copy(side):
        n, where, _ = sides[side]
        return pltpu.make_async_remote_copy(
            src_ref=weights.at[1],
            dst_ref=weights.at[2 - 2 * n],
            send_sem=weight_send.at[n],
            recv_sem=weight_recv.at[n],
            device_id=(where, tower),
            device_id_type=MESH,
        )

    def line_copy(k, source):
        there, where = line_peer(k)
        return pltpu.make_async_remote_copy(
            src_ref=tallies,
            dst_ref=line_sums.at[source],
            send_sem=line_send.at[k],
            recv_sem=line_recv.at[source],
            device_id=where,
            device_id_type=MESH,
        )

    def all_copy(k, source):
        there, where = all_peer(k)
        return pltpu.make_async_remote_copy(
            src_ref=tallies,
            dst_ref=all_sums.at[source],
            send_sem=all_send.at[k],
            recv_sem=all_recv.at[source],
            device_id=where,
            device_id_type=MESH,
        )

    for a in range(2):
        for c in range(CHUNKS):
            x_copy(a, c).start()
        for side in range(2):
            own_copy(a, side).start()
    weights[1] = jnp.broadcast_to(weight_in[...].astype(F32), (8, SUPER))
    for side in range(2):
        weight_copy(side).start()

    scale = jnp.exp(jnp.full((1, 128), exponent[0], F32))[:, 0:1]
    scale2 = scale * LOG2E
    shift2 = offset[0] * LOG2E

    txt_grad[...] = jnp.zeros_like(txt_grad)
    txt_along[...] = jnp.zeros_like(txt_along)
    tallies[...] = jnp.zeros_like(tallies)
    for load in loads:
        load.wait()

    def norms(a, slot, c):
        wide = held[a, :, columns_of(slot, c)].astype(F32)
        total = jnp.sum(wide * wide, axis=0, keepdims=True)
        inverse = lax.rsqrt(total + 1e-06)
        here = pl.ds(pl.multiple_of(c * CHUNK, CHUNK), CHUNK)
        inv_row[a, slot, :, here] = jnp.broadcast_to(inverse, (8, CHUNK))
        if slot == 1:
            inv_col[a, here, :] = jnp.transpose(jnp.broadcast_to(inverse, (128, CHUNK)))

    def forward(a, c):
        x_copy(a, c).wait_recv()
        for side in range(2):
            other_copy(a, side, c).start()

    def from_sides(a, c):
        for side in range(2):

            @pl.when(c == 0)
            def _():
                own_copy(a, 1 - side).wait_recv()

            other_copy(a, 1 - side, c).wait_recv()
            norms(a, 2 * side, c)

    def text_step(c, carry):
        forward(TXT, c)
        norms(TXT, 1, c)
        here = pl.ds(pl.multiple_of(c * CHUNK, CHUNK), CHUNK)
        turned_txt[here, :] = jnp.transpose(held[TXT, :, columns_of(1, c)])
        from_sides(TXT, c)
        return carry

    lax.fori_loop(0, CHUNKS, text_step, 0)
    for side in range(2):
        weight_copy(1 - side).wait_recv()

    def image_out_copy(c):
        here = pl.ds(pl.multiple_of(c * CHUNK, CHUNK), CHUNK)
        return pltpu.make_async_copy(staged.at[IMG, :, here], img_out.at[:, here], out_sem.at[c])

    def image_rows(c):
        half = c // 2
        here = pl.ds(pl.multiple_of(c * CHUNK, CHUNK), CHUNK)
        turned_img[...] = jnp.transpose(held[IMG, :, columns_of(1, c)])
        row_scale = inv_col[IMG, here, 0:1] * scale2
        along = jnp.zeros((CHUNK, 128), F32)
        bias = jnp.zeros((CHUNK, 128), F32)
        loss = jnp.zeros((CHUNK, 128), F32)
        for j in range(5):
            begin = pl.multiple_of(half * BLOCK + j * BLOCK, BLOCK)
            slot, inside = begin // SUPER, lax.rem(begin, SUPER)
            inv_text = inv_row[TXT, slot, 0:1, pl.ds(pl.multiple_of(inside, BLOCK), BLOCK)]
            product = jnp.dot(
                turned_img[...], held[TXT, :, pl.ds(begin, BLOCK)], preferred_element_type=F32
            )
            logits2 = product * inv_text * row_scale + shift2
            grown = jnp.exp2(logits2)
            more = grown + 1.0
            sig = grown / more
            loss = loss + fold(jnp.log(more[:, :CHUNK] * more[:, CHUNK:]))
            if j == 2:
                mine = lax.broadcasted_iota(jnp.int32, (CHUNK, BLOCK), 0) + lax.rem(c, 2) * CHUNK
                match = mine == lax.broadcasted_iota(jnp.int32, (CHUNK, BLOCK), 1)
                sig = jnp.where(match, sig - 1.0, sig)
                loss = loss - fold(jnp.where(match, logits2, 0.0)) * (1.0 / LOG2E)
            scaled = sig * inv_text
            along = along + fold(scaled * product)
            bias = bias + fold(sig)
            coef[:, pl.ds(j * BLOCK, BLOCK)] = scaled.astype(BF16)
        band = pl.ds(pl.multiple_of(half * BLOCK, BLOCK), 5 * BLOCK)
        grad = lax.dot_general(
            held[TXT, pl.ds(0, PART), band],
            coef[...],
            (((1,), (1,)), ((), ())),
            preferred_element_type=F32,
        )
        weight = weights[1, 0:1, here]
        inverse = inv_row[IMG, 1, 0:1, here]
        along_row = row_of(along) * inverse
        wide = held[IMG, pl.ds(0, PART), columns_of(1, c)].astype(F32)
        result = (weight * inverse * scale) * (grad - wide * (inverse * along_row))
        staged[IMG, :, here] = result.astype(BF16)
        image_out_copy(c).start()
        for n, value in enumerate((row_of(loss), scale * along_row, row_of(bias))):
            total = jnp.sum(weight * value, axis=1, keepdims=True)
            tallies[n : n + 1, :] += jnp.broadcast_to(total, (1, 128))

    def text_rows(slot, c, block, diagonal):
        rows = pl.ds(pl.multiple_of(block * BLOCK, BLOCK), BLOCK)
        here = pl.ds(pl.multiple_of(c * CHUNK, CHUNK), CHUNK)
        there = columns_of(slot, c)
        inv_image = inv_row[IMG, slot, 0:1, here]
        heavy = inv_image * weights[slot, 0:1, here]
        row_scale = inv_col[TXT, rows, 0:1] * scale2
        product = jnp.dot(turned_txt[rows, :], held[IMG, :, there], preferred_element_type=F32)
        grown = jnp.exp2(product * inv_image * row_scale + shift2)
        sig = grown / (grown + 1.0)
        if diagonal:
            mine = lax.broadcasted_iota(jnp.int32, (BLOCK, CHUNK), 0) + block * BLOCK
            other = lax.broadcasted_iota(jnp.int32, (BLOCK, CHUNK), 1) + c * CHUNK
            sig = jnp.where(mine == other, sig - 1.0, sig)
        scaled = sig * heavy
        txt_along[rows, :] += fold(scaled * product)
        txt_grad[:, rows] += lax.dot_general(
            held[IMG, pl.ds(0, PART), there],
            scaled.astype(BF16),
            (((1,), (1,)), ((), ())),
            preferred_element_type=F32,
        )

    def image_step(c, carry):
        forward(IMG, c)
        norms(IMG, 1, c)
        image_rows(c)

        @pl.when(c == CHUNKS - 1)
        def _():
            def send(k, carry):
                line_copy(k, rank).start()
                return carry

            lax.fori_loop(1, 2 * LINE, send, 0)

        text_rows(1, c, 0, True)
        text_rows(1, c, 1, True)
        from_sides(IMG, c)
        text_rows(0, c, 0, False)
        text_rows(2, c, 1, False)
        late = c >= CHUNKS // 2
        text_rows(jnp.where(late, 0, 2), c, jnp.where(late, 1, 0), False)
        return carry

    lax.fori_loop(0, CHUNKS, image_step, 0)

    def line_wait(k, carry):
        copy = line_copy(k, line_peer(k)[0])
        copy.wait_recv()
        copy.wait_send()
        return carry

    line_sums[rank] = tallies[...]
    lax.fori_loop(1, 2 * LINE, line_wait, 0)
    total = line_sums[0]
    for k in range(1, 2 * LINE):
        total = total + line_sums[k]
    tallies[...] = total
    all_sums[line] = total

    def all_send_one(k, carry):
        all_copy(k, line).start()
        return carry

    lax.fori_loop(1, lines, all_send_one, 0)

    def text_out_copy(c):
        here = pl.ds(c * CHUNK, CHUNK)
        return pltpu.make_async_copy(
            staged.at[TXT, :, here], txt_out.at[:, here], out_sem.at[CHUNKS + c]
        )

    for c in range(CHUNKS):
        here = pl.ds(c * CHUNK, CHUNK)
        inverse = inv_row[TXT, 1, 0:1, here]
        along_row = row_of(txt_along[here, :]) * inverse
        wide = held[TXT, pl.ds(0, PART), columns_of(1, c)].astype(F32)
        result = (inverse * scale) * (txt_grad[:, here] - wide * (inverse * along_row))
        staged[TXT, :, here] = result.astype(BF16)
        text_out_copy(c).start()

    def all_wait(k, carry):
        copy = all_copy(k, all_peer(k)[0])
        copy.wait_recv()
        copy.wait_send()
        return carry

    lax.fori_loop(1, lines, all_wait, 0)
    total = all_sums[0]
    for k in range(1, lines):
        total = total + all_sums[k]
    sums_out[...] = total * (1.0 / (2.0 * count * SUPER * 5 * BLOCK))

    for c in range(CHUNKS):
        image_out_copy(c).wait()
        text_out_copy(c).wait()
    for a in range(2):
        for side in range(2):
            own_copy(a, side).wait_send()
        for c in range(CHUNKS):
            x_copy(a, c).wait_send()
            for side in range(2):
                other_copy(a, side, c).wait_send()
    for side in range(2):
        weight_copy(side).wait_send()


def shards(count, vision, caption, importance, scale_exponent, similarity_shift):
    lines = count // LINE
    dma = pltpu.SemaphoreType.DMA
    hbm, vmem = pl.BlockSpec(memory_space=pl.ANY), pl.BlockSpec(memory_space=pltpu.VMEM)
    smem = pl.BlockSpec(memory_space=pltpu.SMEM)
    img_out, txt_out, sums = pl.pallas_call(
        functools.partial(kernel, count),
        out_shape=(
            jax.ShapeDtypeStruct((PART, SUPER), BF16),
            jax.ShapeDtypeStruct((PART, SUPER), BF16),
            jax.ShapeDtypeStruct((8, 128), F32),
        ),
        in_specs=[hbm, hbm, vmem, smem, smem],
        out_specs=(hbm, hbm, vmem),
        scratch_shapes=[
            pltpu.VMEM((2, FULL, 3 * SUPER), BF16),
            pltpu.VMEM((3, 8, SUPER), F32),
            pltpu.VMEM((2, 3, 8, SUPER), F32),
            pltpu.VMEM((2, SUPER, 128), F32),
            pltpu.VMEM((SUPER, FULL), BF16),
            pltpu.VMEM((CHUNK, FULL), BF16),
            pltpu.VMEM((PART, SUPER), F32),
            pltpu.VMEM((SUPER, 128), F32),
            pltpu.VMEM((8, 128), F32),
            pltpu.VMEM((2, PART, SUPER), BF16),
            pltpu.VMEM((CHUNK, 5 * BLOCK), BF16),
            pltpu.VMEM((2 * LINE, 8, 128), F32),
            pltpu.VMEM((lines, 8, 128), F32),
            dma((2,)),
            dma((2, CHUNKS)),
            dma((2, CHUNKS)),
            dma((2, 2)),
            dma((2, 2)),
            dma((2, 2, CHUNKS)),
            dma((2, 2, CHUNKS)),
            dma((2,)),
            dma((2,)),
            dma((2 * CHUNKS,)),
            dma((2 * LINE,)),
            dma((2 * LINE,)),
            dma((lines,)),
            dma((lines,)),
        ],
        compiler_params=pltpu.CompilerParams(
            collective_id=0, has_side_effects=True, vmem_limit_bytes=60 * 2**20
        ),
        name="band",
    )(caption.T, vision.T, importance.reshape(1, SUPER), scale_exponent, similarity_shift)
    return img_out.T, txt_out.T, sums[:3, 0]


def solution(mesh):
    in_specs = (P("blk", "tower"), P("blk", "tower"), P("blk"), P(), P())
    out_specs = (P("blk", "tower"), P("blk", "tower"), P())
    return jax.shard_map(
        functools.partial(shards, mesh.shape["blk"]),
        mesh=mesh,
        in_specs=in_specs,
        out_specs=out_specs,
        check_vma=False,
    )
```

```python
import functools
import math

import jax
import jax.numpy as jnp
from jax import lax
from jax.experimental import pallas as pl
from jax.experimental.pallas import tpu as pltpu
from jax.sharding import PartitionSpec as P

MESH = pl.DeviceIdType.MESH
F32, BF16 = jnp.float32, jnp.bfloat16
TXT, IMG = 0, 1
BLOCK = 512
SUPER = 1024
PART = 576
FULL = 1152
CHUNK = 256
CHUNKS = SUPER // CHUNK
AHEAD = 2
LINE = 8
LOG2E = math.log2(math.e)


def fold(v):
    total = v[:, :128]
    for k in range(1, v.shape[1] // 128):
        total = total + v[:, 128 * k : 128 * (k + 1)]
    return total


def row_of(partial):
    return jnp.sum(jnp.transpose(partial), axis=0, keepdims=True)


def kernel(
    count,
    txt_in,
    img_in,
    weight_in,
    exponent,
    offset,
    img_out,
    txt_out,
    sums_out,
    held,
    weights,
    inv_row,
    inv_col,
    turned_txt,
    turned_img,
    txt_grad,
    txt_along,
    tallies,
    staged,
    coef,
    line_sums,
    all_sums,
    load_sem,
    x_send,
    x_recv,
    own_send,
    own_recv,
    other_send,
    other_recv,
    weight_send,
    weight_recv,
    out_sem,
    line_send,
    line_recv,
    all_send,
    all_recv,
):
    sb = lax.axis_index("blk")
    tower = lax.axis_index("tower")
    away = 1 - tower
    left, right = lax.rem(sb + count - 1, count), lax.rem(sb + 1, count)
    place, line = lax.rem(sb, LINE), sb // LINE
    lines = count // LINE
    rank = place * 2 + tower
    left_end, right_end = place == 0, place == LINE - 1
    inputs = (txt_in, img_in)
    sides = ((0, left, left_end), (1, right, right_end))

    def line_peer(k):
        there = lax.rem(rank + k, 2 * LINE)
        return there, (line * LINE + there // 2, lax.rem(there, 2))

    def all_peer(k):
        there = lax.rem(line + k, lines)
        return there, (there * LINE + place, tower)

    def columns_of(slot, c):
        return pl.ds(pl.multiple_of(slot * SUPER + c * CHUNK, CHUNK), CHUNK)

    def whole(slot):
        return pl.ds(slot * SUPER, SUPER)

    loads = []
    for a in range(2):
        target = held.at[a, pl.ds(0, PART), whole(1)]
        loads.append(pltpu.make_async_copy(inputs[a], target, load_sem.at[a]))
        loads[a].start()

    barrier = pltpu.get_barrier_semaphore()

    def greet(where):
        pl.semaphore_signal(barrier, inc=1, device_id=where, device_id_type=MESH)

    for where in ((sb, away), (left, tower), (right, tower)):
        greet(where)

    @pl.when(left_end)
    def _():
        greet((left, away))

    @pl.when(right_end)
    def _():
        greet((right, away))

    def greet_line(k, carry):
        greet(line_peer(k)[1])
        return carry

    def greet_all(k, carry):
        greet(all_peer(k)[1])
        return carry

    lax.fori_loop(1, 2 * LINE, greet_line, 0)
    lax.fori_loop(1, lines, greet_all, 0)
    at_end = jnp.logical_or(left_end, right_end)
    pl.semaphore_wait(barrier, jnp.where(at_end, 4, 3) + (2 * LINE - 1) + (lines - 1))

    def x_copy(a, c):
        return pltpu.make_async_remote_copy(
            src_ref=inputs[a].at[:, pl.ds(c * CHUNK, CHUNK)],
            dst_ref=held.at[a, pl.ds(PART, PART), columns_of(1, c)],
            send_sem=x_send.at[a, c],
            recv_sem=x_recv.at[a, c],
            device_id=(sb, away),
            device_id_type=MESH,
        )

    def own_copy(a, side, c):
        n, where, _ = sides[side]
        return pltpu.make_async_remote_copy(
            src_ref=inputs[a].at[:, pl.ds(c * CHUNK, CHUNK)],
            dst_ref=held.at[a, pl.ds(0, PART), columns_of(2 - 2 * n, c)],
            send_sem=own_send.at[a, n, c],
            recv_sem=own_recv.at[a, n, c],
            device_id=(where, tower),
            device_id_type=MESH,
        )

    def other_copy(a, side, c, cross=False):
        n, where, _ = sides[side]
        here = pl.ds(c * CHUNK, CHUNK)
        return pltpu.make_async_remote_copy(
            src_ref=inputs[a].at[:, here] if cross else held.at[a, pl.ds(PART, PART), columns_of(1, c)],
            dst_ref=held.at[a, pl.ds(PART, PART), columns_of(2 - 2 * n, c)],
            send_sem=other_send.at[a, n, c],
            recv_sem=other_recv.at[a, n, c],
            device_id=(where, away if cross else tower),
            device_id_type=MESH,
        )

    def begin(a, c):
        x_copy(a, c).start()
        for side in range(2):
            own_copy(a, side, c).start()

            @pl.when(sides[side][2])
            def _():
                other_copy(a, side, c, cross=True).start()

    def weight_copy(side):
        n, where, _ = sides[side]
        return pltpu.make_async_remote_copy(
            src_ref=weights.at[1],
            dst_ref=weights.at[2 - 2 * n],
            send_sem=weight_send.at[n],
            recv_sem=weight_recv.at[n],
            device_id=(where, tower),
            device_id_type=MESH,
        )

    def line_copy(k, source):
        there, where = line_peer(k)
        return pltpu.make_async_remote_copy(
            src_ref=tallies,
            dst_ref=line_sums.at[source],
            send_sem=line_send.at[k],
            recv_sem=line_recv.at[source],
            device_id=where,
            device_id_type=MESH,
        )

    def all_copy(k, source):
        there, where = all_peer(k)
        return pltpu.make_async_remote_copy(
            src_ref=tallies,
            dst_ref=all_sums.at[source],
            send_sem=all_send.at[k],
            recv_sem=all_recv.at[source],
            device_id=where,
            device_id_type=MESH,
        )

    for c in range(AHEAD):
        begin(TXT, c)
    weights[1] = jnp.broadcast_to(weight_in[...].astype(F32), (8, SUPER))
    for side in range(2):
        weight_copy(side).start()

    scale = jnp.exp(jnp.full((1, 128), exponent[0], F32))[:, 0:1]
    scale2 = scale * LOG2E
    shift2 = offset[0] * LOG2E

    txt_grad[...] = jnp.zeros_like(txt_grad)
    txt_along[...] = jnp.zeros_like(txt_along)
    tallies[...] = jnp.zeros_like(tallies)
    for load in loads:
        load.wait()

    def norms(a, slot, c):
        wide = held[a, :, columns_of(slot, c)].astype(F32)
        total = jnp.sum(wide * wide, axis=0, keepdims=True)
        inverse = lax.rsqrt(total + 1e-06)
        here = pl.ds(pl.multiple_of(c * CHUNK, CHUNK), CHUNK)
        inv_row[a, slot, :, here] = jnp.broadcast_to(inverse, (8, CHUNK))
        if slot == 1:
            inv_col[a, here, :] = jnp.transpose(jnp.broadcast_to(inverse, (128, CHUNK)))

    def forward(a, c):
        x_copy(a, c).wait_recv()
        for side in range(2):

            @pl.when(jnp.logical_not(sides[side][2]))
            def _():
                other_copy(a, side, c).start()

        @pl.when(c < CHUNKS - AHEAD)
        def _():
            begin(a, c + AHEAD)

        if a == TXT:

            @pl.when(c >= CHUNKS - AHEAD)
            def _():
                begin(IMG, c - (CHUNKS - AHEAD))

    def from_sides(a, c):
        for side in range(2):
            own_copy(a, 1 - side, c).wait_recv()
            other_copy(a, 1 - side, c).wait_recv()
            norms(a, 2 * side, c)

    def text_step(c, carry):
        forward(TXT, c)
        norms(TXT, 1, c)
        here = pl.ds(pl.multiple_of(c * CHUNK, CHUNK), CHUNK)
        turned_txt[here, :] = jnp.transpose(held[TXT, :, columns_of(1, c)])

        @pl.when(c > 0)
        def _():
            from_sides(TXT, c - 1)

        return carry

    lax.fori_loop(0, CHUNKS, text_step, 0)
    for side in range(2):
        weight_copy(1 - side).wait_recv()

    def image_out_copy(c):
        here = pl.ds(pl.multiple_of(c * CHUNK, CHUNK), CHUNK)
        return pltpu.make_async_copy(staged.at[IMG, :, here], img_out.at[:, here], out_sem.at[c])

    def image_rows(c):
        half = c // 2
        here = pl.ds(pl.multiple_of(c * CHUNK, CHUNK), CHUNK)
        turned_img[...] = jnp.transpose(held[IMG, :, columns_of(1, c)])
        row_scale = inv_col[IMG, here, 0:1] * scale2
        along = jnp.zeros((CHUNK, 128), F32)
        bias = jnp.zeros((CHUNK, 128), F32)
        loss = jnp.zeros((CHUNK, 128), F32)
        for j in range(5):
            begin = pl.multiple_of(half * BLOCK + j * BLOCK, BLOCK)
            slot, inside = begin // SUPER, lax.rem(begin, SUPER)
            inv_text = inv_row[TXT, slot, 0:1, pl.ds(pl.multiple_of(inside, BLOCK), BLOCK)]
            product = jnp.dot(
                turned_img[...], held[TXT, :, pl.ds(begin, BLOCK)], preferred_element_type=F32
            )
            logits2 = product * inv_text * row_scale + shift2
            grown = jnp.exp2(logits2)
            more = grown + 1.0
            sig = grown / more
            loss = loss + fold(jnp.log(more[:, :CHUNK] * more[:, CHUNK:]))
            if j == 2:
                mine = lax.broadcasted_iota(jnp.int32, (CHUNK, BLOCK), 0) + lax.rem(c, 2) * CHUNK
                match = mine == lax.broadcasted_iota(jnp.int32, (CHUNK, BLOCK), 1)
                sig = jnp.where(match, sig - 1.0, sig)
                loss = loss - fold(jnp.where(match, logits2, 0.0)) * (1.0 / LOG2E)
            scaled = sig * inv_text
            along = along + fold(scaled * product)
            bias = bias + fold(sig)
            coef[:, pl.ds(j * BLOCK, BLOCK)] = scaled.astype(BF16)
        band = pl.ds(pl.multiple_of(half * BLOCK, BLOCK), 5 * BLOCK)
        grad = lax.dot_general(
            held[TXT, pl.ds(0, PART), band],
            coef[...],
            (((1,), (1,)), ((), ())),
            preferred_element_type=F32,
        )
        weight = weights[1, 0:1, here]
        inverse = inv_row[IMG, 1, 0:1, here]
        along_row = row_of(along) * inverse
        wide = held[IMG, pl.ds(0, PART), columns_of(1, c)].astype(F32)
        result = (weight * inverse * scale) * (grad - wide * (inverse * along_row))
        staged[IMG, :, here] = result.astype(BF16)
        image_out_copy(c).start()
        for n, value in enumerate((row_of(loss), scale * along_row, row_of(bias))):
            total = jnp.sum(weight * value, axis=1, keepdims=True)
            tallies[n : n + 1, :] += jnp.broadcast_to(total, (1, 128))

    def text_rows(slot, c, block, diagonal):
        rows = pl.ds(pl.multiple_of(block * BLOCK, BLOCK), BLOCK)
        here = pl.ds(pl.multiple_of(c * CHUNK, CHUNK), CHUNK)
        there = columns_of(slot, c)
        inv_image = inv_row[IMG, slot, 0:1, here]
        heavy = inv_image * weights[slot, 0:1, here]
        row_scale = inv_col[TXT, rows, 0:1] * scale2
        product = jnp.dot(turned_txt[rows, :], held[IMG, :, there], preferred_element_type=F32)
        grown = jnp.exp2(product * inv_image * row_scale + shift2)
        sig = grown / (grown + 1.0)
        if diagonal:
            mine = lax.broadcasted_iota(jnp.int32, (BLOCK, CHUNK), 0) + block * BLOCK
            other = lax.broadcasted_iota(jnp.int32, (BLOCK, CHUNK), 1) + c * CHUNK
            sig = jnp.where(mine == other, sig - 1.0, sig)
        scaled = sig * heavy
        txt_along[rows, :] += fold(scaled * product)
        txt_grad[:, rows] += lax.dot_general(
            held[IMG, pl.ds(0, PART), there],
            scaled.astype(BF16),
            (((1,), (1,)), ((), ())),
            preferred_element_type=F32,
        )

    def image_step(c, carry):
        forward(IMG, c)
        norms(IMG, 1, c)

        @pl.when(c == 0)
        def _():
            from_sides(TXT, CHUNKS - 1)

        image_rows(c)

        @pl.when(c == CHUNKS - 1)
        def _():
            def send(k, carry):
                line_copy(k, rank).start()
                return carry

            lax.fori_loop(1, 2 * LINE, send, 0)

        text_rows(1, c, 0, True)
        text_rows(1, c, 1, True)
        from_sides(IMG, c)
        text_rows(0, c, 0, False)
        text_rows(2, c, 1, False)
        late = c >= CHUNKS // 2
        text_rows(jnp.where(late, 0, 2), c, jnp.where(late, 1, 0), False)
        return carry

    lax.fori_loop(0, CHUNKS, image_step, 0)

    def line_wait(k, carry):
        copy = line_copy(k, line_peer(k)[0])
        copy.wait_recv()
        copy.wait_send()
        return carry

    line_sums[rank] = tallies[...]
    lax.fori_loop(1, 2 * LINE, line_wait, 0)
    total = line_sums[0]
    for k in range(1, 2 * LINE):
        total = total + line_sums[k]
    tallies[...] = total
    all_sums[line] = total

    def all_send_one(k, carry):
        all_copy(k, line).start()
        return carry

    lax.fori_loop(1, lines, all_send_one, 0)

    def text_out_copy(c):
        here = pl.ds(c * CHUNK, CHUNK)
        return pltpu.make_async_copy(
            staged.at[TXT, :, here], txt_out.at[:, here], out_sem.at[CHUNKS + c]
        )

    for c in range(CHUNKS):
        here = pl.ds(c * CHUNK, CHUNK)
        inverse = inv_row[TXT, 1, 0:1, here]
        along_row = row_of(txt_along[here, :]) * inverse
        wide = held[TXT, pl.ds(0, PART), columns_of(1, c)].astype(F32)
        result = (inverse * scale) * (txt_grad[:, here] - wide * (inverse * along_row))
        staged[TXT, :, here] = result.astype(BF16)
        text_out_copy(c).start()

    def all_wait(k, carry):
        copy = all_copy(k, all_peer(k)[0])
        copy.wait_recv()
        copy.wait_send()
        return carry

    lax.fori_loop(1, lines, all_wait, 0)
    total = all_sums[0]
    for k in range(1, lines):
        total = total + all_sums[k]
    sums_out[...] = total * (1.0 / (2.0 * count * SUPER * 5 * BLOCK))

    for c in range(CHUNKS):
        image_out_copy(c).wait()
        text_out_copy(c).wait()
    for a in range(2):
        for c in range(CHUNKS):
            x_copy(a, c).wait_send()
            for side in range(2):
                own_copy(a, side, c).wait_send()
                other_copy(a, side, c).wait_send()
    for side in range(2):
        weight_copy(side).wait_send()


def shards(count, vision, caption, importance, scale_exponent, similarity_shift):
    lines = count // LINE
    dma = pltpu.SemaphoreType.DMA
    hbm, vmem = pl.BlockSpec(memory_space=pl.ANY), pl.BlockSpec(memory_space=pltpu.VMEM)
    smem = pl.BlockSpec(memory_space=pltpu.SMEM)
    img_out, txt_out, sums = pl.pallas_call(
        functools.partial(kernel, count),
        out_shape=(
            jax.ShapeDtypeStruct((PART, SUPER), BF16),
            jax.ShapeDtypeStruct((PART, SUPER), BF16),
            jax.ShapeDtypeStruct((8, 128), F32),
        ),
        in_specs=[hbm, hbm, vmem, smem, smem],
        out_specs=(hbm, hbm, vmem),
        scratch_shapes=[
            pltpu.VMEM((2, FULL, 3 * SUPER), BF16),
            pltpu.VMEM((3, 8, SUPER), F32),
            pltpu.VMEM((2, 3, 8, SUPER), F32),
            pltpu.VMEM((2, SUPER, 128), F32),
            pltpu.VMEM((SUPER, FULL), BF16),
            pltpu.VMEM((CHUNK, FULL), BF16),
            pltpu.VMEM((PART, SUPER), F32),
            pltpu.VMEM((SUPER, 128), F32),
            pltpu.VMEM((8, 128), F32),
            pltpu.VMEM((2, PART, SUPER), BF16),
            pltpu.VMEM((CHUNK, 5 * BLOCK), BF16),
            pltpu.VMEM((2 * LINE, 8, 128), F32),
            pltpu.VMEM((lines, 8, 128), F32),
            dma((2,)),
            dma((2, CHUNKS)),
            dma((2, CHUNKS)),
            dma((2, 2, CHUNKS)),
            dma((2, 2, CHUNKS)),
            dma((2, 2, CHUNKS)),
            dma((2, 2, CHUNKS)),
            dma((2,)),
            dma((2,)),
            dma((2 * CHUNKS,)),
            dma((2 * LINE,)),
            dma((2 * LINE,)),
            dma((lines,)),
            dma((lines,)),
        ],
        compiler_params=pltpu.CompilerParams(
            collective_id=0, has_side_effects=True, vmem_limit_bytes=60 * 2**20
        ),
        name="band",
    )(caption.T, vision.T, importance.reshape(1, SUPER), scale_exponent, similarity_shift)
    return img_out.T, txt_out.T, sums[:3, 0]


def solution(mesh):
    in_specs = (P("blk", "tower"), P("blk", "tower"), P("blk"), P(), P())
    out_specs = (P("blk", "tower"), P("blk", "tower"), P())
    return jax.shard_map(
        functools.partial(shards, mesh.shape["blk"]),
        mesh=mesh,
        in_specs=in_specs,
        out_specs=out_specs,
        check_vma=False,
    )
```

```python
import functools
import math

import jax
import jax.numpy as jnp
from jax import lax
from jax.experimental import pallas as pl
from jax.experimental.pallas import tpu as pltpu
from jax.sharding import PartitionSpec as P

MESH = pl.DeviceIdType.MESH
F32, BF16 = jnp.float32, jnp.bfloat16
TXT, IMG = 0, 1
BLOCK = 512
SUPER = 1024
PART = 576
FULL = 1152
CHUNK = 256
CHUNKS = SUPER // CHUNK
AHEAD = 3
PIECES = 4
LINE = 8
LOG2E = math.log2(math.e)


def fold(v):
    total = v[:, :128]
    for k in range(1, v.shape[1] // 128):
        total = total + v[:, 128 * k : 128 * (k + 1)]
    return total


def row_of(partial):
    return jnp.sum(jnp.transpose(partial), axis=0, keepdims=True)


def kernel(
    count,
    txt_in,
    img_in,
    weight_in,
    exponent,
    offset,
    img_out,
    txt_out,
    sums_out,
    held,
    weights,
    inv_row,
    inv_col,
    turned_txt,
    turned_img,
    txt_grad,
    txt_along,
    tallies,
    staged,
    coef,
    line_sums,
    all_sums,
    load_sem,
    x_send,
    x_recv,
    own_send,
    own_recv,
    other_send,
    other_recv,
    weight_send,
    weight_recv,
    out_sem,
    line_send,
    line_recv,
    all_send,
    all_recv,
):
    sb = lax.axis_index("blk")
    tower = lax.axis_index("tower")
    away = 1 - tower
    left, right = lax.rem(sb + count - 1, count), lax.rem(sb + 1, count)
    place, line = lax.rem(sb, LINE), sb // LINE
    lines = count // LINE
    rank = place * 2 + tower
    left_end, right_end = place == 0, place == LINE - 1
    inputs = (txt_in, img_in)
    sides = ((0, left, left_end), (1, right, right_end))

    def line_peer(k):
        there = lax.rem(rank + k, 2 * LINE)
        return there, (line * LINE + there // 2, lax.rem(there, 2))

    def all_peer(k):
        there = lax.rem(line + k, lines)
        return there, (there * LINE + place, tower)

    def columns_of(slot, c):
        return pl.ds(pl.multiple_of(slot * SUPER + c * CHUNK, CHUNK), CHUNK)

    def whole(slot):
        return pl.ds(slot * SUPER, SUPER)

    loads = []
    for a in range(2):
        target = held.at[a, pl.ds(0, PART), whole(1)]
        loads.append(pltpu.make_async_copy(inputs[a], target, load_sem.at[a]))
        loads[a].start()

    barrier = pltpu.get_barrier_semaphore()

    def greet(where):
        pl.semaphore_signal(barrier, inc=1, device_id=where, device_id_type=MESH)

    for where in ((sb, away), (left, tower), (right, tower)):
        greet(where)

    @pl.when(left_end)
    def _():
        greet((left, away))

    @pl.when(right_end)
    def _():
        greet((right, away))

    def greet_line(k, carry):
        greet(line_peer(k)[1])
        return carry

    def greet_all(k, carry):
        greet(all_peer(k)[1])
        return carry

    lax.fori_loop(1, 2 * LINE, greet_line, 0)
    lax.fori_loop(1, lines, greet_all, 0)
    at_end = jnp.logical_or(left_end, right_end)
    pl.semaphore_wait(barrier, jnp.where(at_end, 4, 3) + (2 * LINE - 1) + (lines - 1))

    def x_copy(a, c):
        return pltpu.make_async_remote_copy(
            src_ref=inputs[a].at[:, pl.ds(c * CHUNK, CHUNK)],
            dst_ref=held.at[a, pl.ds(PART, PART), columns_of(1, c)],
            send_sem=x_send.at[a, c],
            recv_sem=x_recv.at[a, c],
            device_id=(sb, away),
            device_id_type=MESH,
        )

    def own_copy(a, side, c):
        n, where, _ = sides[side]
        return pltpu.make_async_remote_copy(
            src_ref=inputs[a].at[:, pl.ds(c * CHUNK, CHUNK)],
            dst_ref=held.at[a, pl.ds(0, PART), columns_of(2 - 2 * n, c)],
            send_sem=own_send.at[a, n, c],
            recv_sem=own_recv.at[a, n, c],
            device_id=(where, tower),
            device_id_type=MESH,
        )

    def other_copy(a, side, c, cross=False):
        n, where, _ = sides[side]
        here = pl.ds(c * CHUNK, CHUNK)
        return pltpu.make_async_remote_copy(
            src_ref=inputs[a].at[:, here] if cross else held.at[a, pl.ds(PART, PART), columns_of(1, c)],
            dst_ref=held.at[a, pl.ds(PART, PART), columns_of(2 - 2 * n, c)],
            send_sem=other_send.at[a, n, c],
            recv_sem=other_recv.at[a, n, c],
            device_id=(where, away if cross else tower),
            device_id_type=MESH,
        )

    def begin(a, c):
        x_copy(a, c).start()
        for side in range(2):
            own_copy(a, side, c).start()

            @pl.when(sides[side][2])
            def _():
                other_copy(a, side, c, cross=True).start()

    def weight_copy(side):
        n, where, _ = sides[side]
        return pltpu.make_async_remote_copy(
            src_ref=weights.at[1],
            dst_ref=weights.at[2 - 2 * n],
            send_sem=weight_send.at[n],
            recv_sem=weight_recv.at[n],
            device_id=(where, tower),
            device_id_type=MESH,
        )

    def line_copy(k, source):
        there, where = line_peer(k)
        return pltpu.make_async_remote_copy(
            src_ref=tallies,
            dst_ref=line_sums.at[source],
            send_sem=line_send.at[k],
            recv_sem=line_recv.at[source],
            device_id=where,
            device_id_type=MESH,
        )

    def all_copy(k, source):
        there, where = all_peer(k)
        return pltpu.make_async_remote_copy(
            src_ref=tallies,
            dst_ref=all_sums.at[source],
            send_sem=all_send.at[k],
            recv_sem=all_recv.at[source],
            device_id=where,
            device_id_type=MESH,
        )

    for c in range(AHEAD):
        begin(TXT, c)
    heavy = weight_in[...].astype(F32)
    for k in range(8):
        weights[1, :, 128 * k : 128 * (k + 1)] = jnp.broadcast_to(heavy[k : k + 1], (8, 128))
    for side in range(2):
        weight_copy(side).start()

    scale = jnp.exp(jnp.full((1, 128), exponent[0], F32))[:, 0:1]
    scale2 = scale * LOG2E
    shift2 = offset[0] * LOG2E

    txt_grad[...] = jnp.zeros_like(txt_grad)
    txt_along[...] = jnp.zeros_like(txt_along)
    tallies[...] = jnp.zeros_like(tallies)
    for load in loads:
        load.wait()

    def norms(a, slot, c):
        wide = held[a, :, columns_of(slot, c)].astype(F32)
        total = jnp.sum(wide * wide, axis=0, keepdims=True)
        inverse = lax.rsqrt(total + 1e-06)
        here = pl.ds(pl.multiple_of(c * CHUNK, CHUNK), CHUNK)
        inv_row[a, slot, :, here] = jnp.broadcast_to(inverse, (8, CHUNK))
        if slot == 1:
            inv_col[a, here, :] = jnp.transpose(jnp.broadcast_to(inverse, (128, CHUNK)))

    def forward(a, c):
        @pl.when(c < CHUNKS - AHEAD)
        def _():
            begin(a, c + AHEAD)

        if a == TXT:

            @pl.when(c >= CHUNKS - AHEAD)
            def _():
                begin(IMG, c - (CHUNKS - AHEAD))

        x_copy(a, c).wait_recv()
        for side in range(2):
            pl.when(jnp.logical_not(sides[side][2]))(other_copy(a, side, c).start)

    def from_sides(a, c):
        for side in range(2):
            own_copy(a, 1 - side, c).wait_recv()
            other_copy(a, 1 - side, c).wait_recv()
            norms(a, 2 * side, c)

    def text_step(c, carry):
        forward(TXT, c)
        norms(TXT, 1, c)
        here = pl.ds(pl.multiple_of(c * CHUNK, CHUNK), CHUNK)
        turned_txt[here, :] = jnp.transpose(held[TXT, :, columns_of(1, c)])

        @pl.when(c > 0)
        def _():
            from_sides(TXT, c - 1)

        return carry

    lax.fori_loop(0, CHUNKS, text_step, 0)
    for side in range(2):
        weight_copy(1 - side).wait_recv()

    def image_out_copy(c):
        here = pl.ds(pl.multiple_of(c * CHUNK, CHUNK), CHUNK)
        return pltpu.make_async_copy(staged.at[IMG, :, here], img_out.at[:, here], out_sem.at[c])

    def image_product(c, j):
        first = pl.multiple_of((c // 2 + j) * BLOCK, BLOCK)
        return jnp.dot(
            turned_img[...], held[TXT, :, pl.ds(first, BLOCK)], preferred_element_type=F32
        )

    def image_coef(c, j, product, sums):
        along, bias, loss = sums
        here = pl.ds(pl.multiple_of(c * CHUNK, CHUNK), CHUNK)
        row_scale = inv_col[IMG, here, 0:1] * scale2
        first = pl.multiple_of((c // 2 + j) * BLOCK, BLOCK)
        slot, inside = first // SUPER, lax.rem(first, SUPER)
        inv_text = inv_row[TXT, slot, 0:1, pl.ds(pl.multiple_of(inside, BLOCK), BLOCK)]
        logits2 = product * inv_text * row_scale + shift2
        grown = jnp.exp2(logits2)
        more = grown + 1.0
        sig = grown / more
        loss = loss + fold(jnp.log(more[:, :CHUNK] * more[:, CHUNK:]))
        if j == 2:
            mine = lax.broadcasted_iota(jnp.int32, (CHUNK, BLOCK), 0) + lax.rem(c, 2) * CHUNK
            match = mine == lax.broadcasted_iota(jnp.int32, (CHUNK, BLOCK), 1)
            sig = jnp.where(match, sig - 1.0, sig)
            loss = loss - fold(jnp.where(match, logits2, 0.0)) * (1.0 / LOG2E)
        scaled = sig * inv_text
        along = along + fold(scaled * product)
        bias = bias + fold(sig)
        coef[:, pl.ds(j * BLOCK, BLOCK)] = scaled.astype(BF16)
        return along, bias, loss

    def image_grad(c, sums):
        along, bias, loss = sums
        here = pl.ds(pl.multiple_of(c * CHUNK, CHUNK), CHUNK)
        band = pl.ds(pl.multiple_of(c // 2 * BLOCK, BLOCK), 5 * BLOCK)
        grad = lax.dot_general(
            held[TXT, pl.ds(0, PART), band],
            coef[...],
            (((1,), (1,)), ((), ())),
            preferred_element_type=F32,
        )
        weight = weights[1, 0:1, here]
        inverse = inv_row[IMG, 1, 0:1, here]
        along_row = row_of(along) * inverse
        wide = held[IMG, pl.ds(0, PART), columns_of(1, c)].astype(F32)
        result = (weight * inverse * scale) * (grad - wide * (inverse * along_row))
        staged[IMG, :, here] = result.astype(BF16)
        image_out_copy(c).start()
        for n, value in enumerate((row_of(loss), scale * along_row, row_of(bias))):
            total = jnp.sum(weight * value, axis=1, keepdims=True)
            tallies[n : n + 1, :] += jnp.broadcast_to(total, (1, 128))

    def text_product(slot, c, block):
        rows = pl.ds(pl.multiple_of(block * BLOCK, BLOCK), BLOCK)
        return jnp.dot(
            turned_txt[rows, :], held[IMG, :, columns_of(slot, c)], preferred_element_type=F32
        )

    def text_coef(slot, c, block, product, diagonal):
        rows = pl.ds(pl.multiple_of(block * BLOCK, BLOCK), BLOCK)
        here = pl.ds(pl.multiple_of(c * CHUNK, CHUNK), CHUNK)
        inv_image = inv_row[IMG, slot, 0:1, here]
        heavy = inv_image * weights[slot, 0:1, here]
        row_scale = inv_col[TXT, rows, 0:1] * scale2
        grown = jnp.exp2(product * inv_image * row_scale + shift2)
        sig = grown / (grown + 1.0)
        if diagonal:
            mine = lax.broadcasted_iota(jnp.int32, (BLOCK, CHUNK), 0) + block * BLOCK
            other = lax.broadcasted_iota(jnp.int32, (BLOCK, CHUNK), 1) + c * CHUNK
            sig = jnp.where(mine == other, sig - 1.0, sig)
        scaled = sig * heavy
        txt_along[rows, :] += fold(scaled * product)
        return scaled.astype(BF16)

    def text_grad(slot, c, block, scaled):
        rows = pl.ds(pl.multiple_of(block * BLOCK, BLOCK), BLOCK)
        txt_grad[:, rows] += lax.dot_general(
            held[IMG, pl.ds(0, PART), columns_of(slot, c)],
            scaled,
            (((1,), (1,)), ((), ())),
            preferred_element_type=F32,
        )

    def own_pairs(c):
        turned_img[...] = jnp.transpose(held[IMG, :, columns_of(1, c)])
        zero = jnp.zeros((CHUNK, 128), F32)
        sums = (zero, zero, zero)
        product = image_product(c, 0)
        for j in range(5):
            after = image_product(c, j + 1) if j < 4 else text_product(1, c, 0)
            sums = image_coef(c, j, product, sums)
            product = after
        after = text_product(1, c, 1)
        image_grad(c, sums)
        scaled = text_coef(1, c, 0, product, True)
        text_grad(1, c, 0, scaled)
        scaled = text_coef(1, c, 1, after, True)
        text_grad(1, c, 1, scaled)

    def side_pairs(c):
        late = c >= CHUNKS // 2
        jobs = [(0, 0), (2, 1), (jnp.where(late, 0, 2), jnp.where(late, 1, 0))]
        product = text_product(jobs[0][0], c, jobs[0][1])
        for n, (slot, block) in enumerate(jobs):
            after = text_product(jobs[n + 1][0], c, jobs[n + 1][1]) if n < 2 else None
            scaled = text_coef(slot, c, block, product, False)
            text_grad(slot, c, block, scaled)
            product = after

    def image_step(c, carry):
        forward(IMG, c)
        norms(IMG, 1, c)

        @pl.when(c == 0)
        def _():
            from_sides(TXT, CHUNKS - 1)

        own_pairs(c)

        @pl.when(c == CHUNKS - 1)
        def _():
            def send(k, carry):
                line_copy(k, rank).start()
                return carry

            lax.fori_loop(1, 2 * LINE, send, 0)

        from_sides(IMG, c)
        side_pairs(c)
        return carry

    lax.fori_loop(0, CHUNKS, image_step, 0)

    def line_wait(k, carry):
        copy = line_copy(k, line_peer(k)[0])
        copy.wait_recv()
        copy.wait_send()
        return carry

    line_sums[rank] = tallies[...]
    lax.fori_loop(1, 2 * LINE, line_wait, 0)
    total = line_sums[0]
    for k in range(1, 2 * LINE):
        total = total + line_sums[k]
    tallies[...] = total
    all_sums[line] = total

    def all_send_one(k, carry):
        all_copy(k, line).start()
        return carry

    lax.fori_loop(1, lines, all_send_one, 0)

    def text_out_copy(c):
        here = pl.ds(c * CHUNK, CHUNK)
        return pltpu.make_async_copy(
            staged.at[TXT, :, here], txt_out.at[:, here], out_sem.at[CHUNKS + c]
        )

    for c in range(CHUNKS):
        here = pl.ds(c * CHUNK, CHUNK)
        inverse = inv_row[TXT, 1, 0:1, here]
        along_row = row_of(txt_along[here, :]) * inverse
        wide = held[TXT, pl.ds(0, PART), columns_of(1, c)].astype(F32)
        result = (inverse * scale) * (txt_grad[:, here] - wide * (inverse * along_row))
        staged[TXT, :, here] = result.astype(BF16)
        text_out_copy(c).start()

    def all_wait(k, carry):
        copy = all_copy(k, all_peer(k)[0])
        copy.wait_recv()
        copy.wait_send()
        return carry

    lax.fori_loop(1, lines, all_wait, 0)
    total = all_sums[0]
    for k in range(1, lines):
        total = total + all_sums[k]
    sums_out[...] = total * (1.0 / (2.0 * count * SUPER * 5 * BLOCK))

    for c in range(CHUNKS):
        image_out_copy(c).wait()
        text_out_copy(c).wait()
    for a in range(2):
        for c in range(CHUNKS):
            x_copy(a, c).wait_send()
            for side in range(2):
                own_copy(a, side, c).wait_send()
                other_copy(a, side, c).wait_send()
    for side in range(2):
        weight_copy(side).wait_send()


def deliver(img_in, txt_in, sums, img_out, txt_out, scalars, held, load_sem, store_sem):
    loads, stores = [], []
    for a, (source, target) in enumerate(((img_in, img_out), (txt_in, txt_out))):
        for k in range(PIECES):
            rows = pl.ds(k * PART // PIECES, PART // PIECES)
            loads.append(pltpu.make_async_copy(source.at[rows], held.at[a, rows], load_sem.at[a, k]))
            stores.append(pltpu.make_async_copy(held.at[a, rows], target.at[rows], store_sem.at[a, k]))
            loads[-1].start()
    for n in range(3):
        scalars[n] = sums[n, 0]
    for load, store in zip(loads, stores):
        load.wait()
        store.start()
    for store in stores:
        store.wait()


def shards(count, vision, caption, importance, scale_exponent, similarity_shift):
    lines = count // LINE
    dma = pltpu.SemaphoreType.DMA
    hbm, vmem = pl.BlockSpec(memory_space=pl.ANY), pl.BlockSpec(memory_space=pltpu.VMEM)
    smem = pl.BlockSpec(memory_space=pltpu.SMEM)
    img_out, txt_out, sums = pl.pallas_call(
        functools.partial(kernel, count),
        out_shape=(
            jax.ShapeDtypeStruct((PART, SUPER), BF16),
            jax.ShapeDtypeStruct((PART, SUPER), BF16),
            jax.ShapeDtypeStruct((8, 128), F32),
        ),
        in_specs=[hbm, hbm, vmem, smem, smem],
        out_specs=(hbm, hbm, vmem),
        scratch_shapes=[
            pltpu.VMEM((2, FULL, 3 * SUPER), BF16),
            pltpu.VMEM((3, 8, SUPER), F32),
            pltpu.VMEM((2, 3, 8, SUPER), F32),
            pltpu.VMEM((2, SUPER, 128), F32),
            pltpu.VMEM((SUPER, FULL), BF16),
            pltpu.VMEM((CHUNK, FULL), BF16),
            pltpu.VMEM((PART, SUPER), F32),
            pltpu.VMEM((SUPER, 128), F32),
            pltpu.VMEM((8, 128), F32),
            pltpu.VMEM((2, PART, SUPER), BF16),
            pltpu.VMEM((CHUNK, 5 * BLOCK), BF16),
            pltpu.VMEM((2 * LINE, 8, 128), F32),
            pltpu.VMEM((lines, 8, 128), F32),
            dma((2,)),
            dma((2, CHUNKS)),
            dma((2, CHUNKS)),
            dma((2, 2, CHUNKS)),
            dma((2, 2, CHUNKS)),
            dma((2, 2, CHUNKS)),
            dma((2, 2, CHUNKS)),
            dma((2,)),
            dma((2,)),
            dma((2 * CHUNKS,)),
            dma((2 * LINE,)),
            dma((2 * LINE,)),
            dma((lines,)),
            dma((lines,)),
        ],
        compiler_params=pltpu.CompilerParams(
            collective_id=0, has_side_effects=True, vmem_limit_bytes=60 * 2**20
        ),
        name="band",
    )(caption.T, vision.T, importance.reshape(8, SUPER // 8), scale_exponent, similarity_shift)
    img_out, txt_out, scalars = pl.pallas_call(
        deliver,
        out_shape=(
            jax.ShapeDtypeStruct((PART, SUPER), BF16),
            jax.ShapeDtypeStruct((PART, SUPER), BF16),
            jax.ShapeDtypeStruct((3,), F32),
        ),
        in_specs=[hbm, hbm, smem],
        out_specs=(hbm, hbm, smem),
        scratch_shapes=[pltpu.VMEM((2, PART, SUPER), BF16), dma((2, PIECES)), dma((2, PIECES))],
        name="deliver",
    )(img_out, txt_out, sums)
    return img_out.T, txt_out.T, scalars


def solution(mesh):
    in_specs = (P("blk", "tower"), P("blk", "tower"), P("blk"), P(), P())
    out_specs = (P("blk", "tower"), P("blk", "tower"), P())
    return jax.shard_map(
        functools.partial(shards, mesh.shape["blk"]),
        mesh=mesh,
        in_specs=in_specs,
        out_specs=out_specs,
        check_vma=False,
    )
```

```python
import functools
import math

import jax
import jax.numpy as jnp
from jax import lax
from jax.experimental import pallas as pl
from jax.experimental.pallas import tpu as pltpu
from jax.sharding import PartitionSpec as P

MESH = pl.DeviceIdType.MESH
F32, BF16 = jnp.float32, jnp.bfloat16
TXT, IMG = 0, 1
BLOCK = 512
SUPER = 1024
PART = 576
FULL = 1152
CHUNK = 256
CHUNKS = SUPER // CHUNK
AHEAD = 1
LINE = 8
LOG2E = math.log2(math.e)


def fold(v):
    total = v[:, :128]
    for k in range(1, v.shape[1] // 128):
        total = total + v[:, 128 * k : 128 * (k + 1)]
    return total


def row_of(partial):
    return jnp.sum(jnp.transpose(partial), axis=0, keepdims=True)


def kernel(
    count,
    txt_in,
    img_in,
    weight_in,
    exponent,
    offset,
    img_out,
    txt_out,
    sums_out,
    held,
    weights,
    inv_row,
    inv_col,
    turned_txt,
    turned_img,
    txt_grad,
    txt_along,
    tallies,
    coef,
    line_sums,
    line_out,
    all_sums,
    load_sem,
    x_send,
    x_recv,
    own_send,
    own_recv,
    other_send,
    other_recv,
    weight_send,
    weight_recv,
    line_send,
    line_recv,
    all_send,
    all_recv,
):
    sb = lax.axis_index("blk")
    tower = lax.axis_index("tower")
    away = 1 - tower
    left, right = lax.rem(sb + count - 1, count), lax.rem(sb + 1, count)
    place, line = lax.rem(sb, LINE), sb // LINE
    lines = count // LINE
    rank = place * 2 + tower
    left_end, right_end = place == 0, place == LINE - 1
    inputs = (txt_in, img_in)
    sides = ((0, left, left_end), (1, right, right_end))

    def line_peer(k):
        there = lax.rem(rank + k, 2 * LINE)
        return there, (line * LINE + there // 2, lax.rem(there, 2))

    def all_peer(k):
        there = lax.rem(line + k, lines)
        return there, (there * LINE + place, tower)

    def columns_of(slot, c):
        return pl.ds(pl.multiple_of(slot * SUPER + c * CHUNK, CHUNK), CHUNK)

    def whole(slot):
        return pl.ds(slot * SUPER, SUPER)

    loads = []
    for a in range(2):
        target = held.at[a, pl.ds(0, PART), whole(1)]
        loads.append(pltpu.make_async_copy(inputs[a], target, load_sem.at[a]))
        loads[a].start()

    barrier = pltpu.get_barrier_semaphore()

    def greet(where):
        pl.semaphore_signal(barrier, inc=1, device_id=where, device_id_type=MESH)

    for where in ((sb, away), (left, tower), (right, tower)):
        greet(where)

    @pl.when(left_end)
    def _():
        greet((left, away))

    @pl.when(right_end)
    def _():
        greet((right, away))

    def greet_line(k, carry):
        greet(line_peer(k)[1])
        return carry

    def greet_all(k, carry):
        greet(all_peer(k)[1])
        return carry

    lax.fori_loop(1, 2 * LINE, greet_line, 0)
    lax.fori_loop(1, lines, greet_all, 0)
    at_end = jnp.logical_or(left_end, right_end)
    pl.semaphore_wait(barrier, jnp.where(at_end, 4, 3) + (2 * LINE - 1) + (lines - 1))

    def x_copy(a, c):
        return pltpu.make_async_remote_copy(
            src_ref=inputs[a].at[:, pl.ds(c * CHUNK, CHUNK)],
            dst_ref=held.at[a, pl.ds(PART, PART), columns_of(1, c)],
            send_sem=x_send.at[a, c],
            recv_sem=x_recv.at[a, c],
            device_id=(sb, away),
            device_id_type=MESH,
        )

    def own_copy(a, side, c):
        n, where, _ = sides[side]
        return pltpu.make_async_remote_copy(
            src_ref=inputs[a].at[:, pl.ds(c * CHUNK, CHUNK)],
            dst_ref=held.at[a, pl.ds(0, PART), columns_of(2 - 2 * n, c)],
            send_sem=own_send.at[a, n, c],
            recv_sem=own_recv.at[a, n, c],
            device_id=(where, tower),
            device_id_type=MESH,
        )

    def other_copy(a, side, c, cross=False):
        n, where, _ = sides[side]
        here = pl.ds(c * CHUNK, CHUNK)
        return pltpu.make_async_remote_copy(
            src_ref=inputs[a].at[:, here] if cross else held.at[a, pl.ds(PART, PART), columns_of(1, c)],
            dst_ref=held.at[a, pl.ds(PART, PART), columns_of(2 - 2 * n, c)],
            send_sem=other_send.at[a, n, c],
            recv_sem=other_recv.at[a, n, c],
            device_id=(where, away if cross else tower),
            device_id_type=MESH,
        )

    def begin(a, c):
        x_copy(a, c).start()
        for side in range(2):
            own_copy(a, side, c).start()

            @pl.when(sides[side][2])
            def _():
                other_copy(a, side, c, cross=True).start()

    def weight_copy(side):
        n, where, _ = sides[side]
        return pltpu.make_async_remote_copy(
            src_ref=weights.at[1],
            dst_ref=weights.at[2 - 2 * n],
            send_sem=weight_send.at[n],
            recv_sem=weight_recv.at[n],
            device_id=(where, tower),
            device_id_type=MESH,
        )

    def line_copy(k, source):
        there, where = line_peer(k)
        return pltpu.make_async_remote_copy(
            src_ref=tallies,
            dst_ref=line_sums.at[source],
            send_sem=line_send.at[k],
            recv_sem=line_recv.at[source],
            device_id=where,
            device_id_type=MESH,
        )

    def all_copy(k, source):
        there, where = all_peer(k)
        return pltpu.make_async_remote_copy(
            src_ref=line_out,
            dst_ref=all_sums.at[source],
            send_sem=all_send.at[k],
            recv_sem=all_recv.at[source],
            device_id=where,
            device_id_type=MESH,
        )

    for c in range(AHEAD):
        begin(TXT, c)
    heavy = weight_in[...].astype(F32)
    for k in range(8):
        weights[1, :, 128 * k : 128 * (k + 1)] = jnp.broadcast_to(heavy[k : k + 1], (8, 128))
    for side in range(2):
        weight_copy(side).start()

    scale = jnp.exp(jnp.full((1, 128), exponent[0], F32))[:, 0:1]
    scale2 = scale * LOG2E
    shift2 = offset[0] * LOG2E

    txt_grad[...] = jnp.zeros_like(txt_grad)
    txt_along[...] = jnp.zeros_like(txt_along)
    tallies[...] = jnp.zeros_like(tallies)
    for load in loads:
        load.wait()

    def norms(a, slot, c):
        wide = held[a, :, columns_of(slot, c)].astype(F32)
        total = jnp.sum(wide * wide, axis=0, keepdims=True)
        inverse = lax.rsqrt(total + 1e-06)
        here = pl.ds(pl.multiple_of(c * CHUNK, CHUNK), CHUNK)
        inv_row[a, slot, :, here] = jnp.broadcast_to(inverse, (8, CHUNK))
        if slot == 1:
            inv_col[a, here, :] = jnp.transpose(jnp.broadcast_to(inverse, (128, CHUNK)))

    def forward(a, c):
        @pl.when(c < CHUNKS - AHEAD)
        def _():
            begin(a, c + AHEAD)

        if a == TXT:

            @pl.when(c >= CHUNKS - AHEAD)
            def _():
                begin(IMG, c - (CHUNKS - AHEAD))

        x_copy(a, c).wait_recv()
        for side in range(2):
            pl.when(jnp.logical_not(sides[side][2]))(other_copy(a, side, c).start)

    def from_sides(a, c):
        for side in range(2):
            own_copy(a, 1 - side, c).wait_recv()
            other_copy(a, 1 - side, c).wait_recv()
            norms(a, 2 * side, c)

    def text_step(c, carry):
        forward(TXT, c)
        norms(TXT, 1, c)
        here = pl.ds(pl.multiple_of(c * CHUNK, CHUNK), CHUNK)
        turned_txt[here, :] = jnp.transpose(held[TXT, :, columns_of(1, c)])

        @pl.when(c > 0)
        def _():
            from_sides(TXT, c - 1)

        return carry

    lax.fori_loop(0, CHUNKS, text_step, 0)
    for side in range(2):
        weight_copy(1 - side).wait_recv()

    def image_product(c, j):
        first = pl.multiple_of((c // 2 + j) * BLOCK, BLOCK)
        return jnp.dot(
            turned_img[...], held[TXT, :, pl.ds(first, BLOCK)], preferred_element_type=F32
        )

    def image_coef(c, j, product, sums):
        along, bias, loss = sums
        here = pl.ds(pl.multiple_of(c * CHUNK, CHUNK), CHUNK)
        row_scale = inv_col[IMG, here, 0:1] * scale2
        first = pl.multiple_of((c // 2 + j) * BLOCK, BLOCK)
        slot, inside = first // SUPER, lax.rem(first, SUPER)
        inv_text = inv_row[TXT, slot, 0:1, pl.ds(pl.multiple_of(inside, BLOCK), BLOCK)]
        logits2 = product * inv_text * row_scale + shift2
        grown = jnp.exp2(logits2)
        more = grown + 1.0
        sig = grown / more
        loss = loss + fold(jnp.log(more[:, :CHUNK] * more[:, CHUNK:]))
        if j == 2:
            mine = lax.broadcasted_iota(jnp.int32, (CHUNK, BLOCK), 0) + lax.rem(c, 2) * CHUNK
            match = mine == lax.broadcasted_iota(jnp.int32, (CHUNK, BLOCK), 1)
            sig = jnp.where(match, sig - 1.0, sig)
            loss = loss - fold(jnp.where(match, logits2, 0.0)) * (1.0 / LOG2E)
        scaled = sig * inv_text
        along = along + fold(scaled * product)
        bias = bias + fold(sig)
        coef[:, pl.ds(j * BLOCK, BLOCK)] = scaled.astype(BF16)
        return along, bias, loss

    def image_grad(c, sums):
        along, bias, loss = sums
        here = pl.ds(pl.multiple_of(c * CHUNK, CHUNK), CHUNK)
        band = pl.ds(pl.multiple_of(c // 2 * BLOCK, BLOCK), 5 * BLOCK)
        grad = lax.dot_general(
            held[TXT, pl.ds(0, PART), band],
            coef[...],
            (((1,), (1,)), ((), ())),
            preferred_element_type=F32,
        )
        weight = weights[1, 0:1, here]
        inverse = inv_row[IMG, 1, 0:1, here]
        along_row = row_of(along) * inverse
        wide = held[IMG, pl.ds(0, PART), columns_of(1, c)].astype(F32)
        result = (weight * inverse * scale) * (grad - wide * (inverse * along_row))
        img_out[:, here] = result.astype(BF16)
        for n, value in enumerate((row_of(loss), scale * along_row, row_of(bias))):
            total = jnp.sum(weight * value, axis=1, keepdims=True)
            tallies[n : n + 1, :] += jnp.broadcast_to(total, (1, 128))

    def text_product(slot, c, block):
        rows = pl.ds(pl.multiple_of(block * BLOCK, BLOCK), BLOCK)
        return jnp.dot(
            turned_txt[rows, :], held[IMG, :, columns_of(slot, c)], preferred_element_type=F32
        )

    def text_coef(slot, c, block, product, diagonal):
        rows = pl.ds(pl.multiple_of(block * BLOCK, BLOCK), BLOCK)
        here = pl.ds(pl.multiple_of(c * CHUNK, CHUNK), CHUNK)
        inv_image = inv_row[IMG, slot, 0:1, here]
        heavy = inv_image * weights[slot, 0:1, here]
        row_scale = inv_col[TXT, rows, 0:1] * scale2
        grown = jnp.exp2(product * inv_image * row_scale + shift2)
        sig = grown / (grown + 1.0)
        if diagonal:
            mine = lax.broadcasted_iota(jnp.int32, (BLOCK, CHUNK), 0) + block * BLOCK
            other = lax.broadcasted_iota(jnp.int32, (BLOCK, CHUNK), 1) + c * CHUNK
            sig = jnp.where(mine == other, sig - 1.0, sig)
        scaled = sig * heavy
        txt_along[rows, :] += fold(scaled * product)
        return scaled.astype(BF16)

    def text_grad(slot, c, block, scaled):
        rows = pl.ds(pl.multiple_of(block * BLOCK, BLOCK), BLOCK)
        txt_grad[:, rows] += lax.dot_general(
            held[IMG, pl.ds(0, PART), columns_of(slot, c)],
            scaled,
            (((1,), (1,)), ((), ())),
            preferred_element_type=F32,
        )

    def own_pairs(c):
        turned_img[...] = jnp.transpose(held[IMG, :, columns_of(1, c)])
        zero = jnp.zeros((CHUNK, 128), F32)
        sums = (zero, zero, zero)
        product = image_product(c, 0)
        for j in range(5):
            after = image_product(c, j + 1) if j < 4 else None
            sums = image_coef(c, j, product, sums)
            product = after
        image_grad(c, sums)

        @pl.when(c == CHUNKS - 1)
        def _():
            for k in range(1, 2 * LINE):
                line_copy(k, rank).start()

        product = text_product(1, c, 0)
        after = text_product(1, c, 1)
        scaled = text_coef(1, c, 0, product, True)
        text_grad(1, c, 0, scaled)
        scaled = text_coef(1, c, 1, after, True)
        text_grad(1, c, 1, scaled)

    def side_pairs(c):
        late = c >= CHUNKS // 2
        jobs = [(0, 0), (2, 1), (jnp.where(late, 0, 2), jnp.where(late, 1, 0))]
        product = text_product(jobs[0][0], c, jobs[0][1])
        for n, (slot, block) in enumerate(jobs):
            after = text_product(jobs[n + 1][0], c, jobs[n + 1][1]) if n < 2 else None
            scaled = text_coef(slot, c, block, product, False)
            text_grad(slot, c, block, scaled)
            product = after

    def line_total():
        line_sums[rank] = tallies[...]
        for k in range(1, 2 * LINE):
            line_copy(k, line_peer(k)[0]).wait_recv()
        total = line_sums[0]
        for k in range(1, 2 * LINE):
            total = total + line_sums[k]
        line_out[...] = total
        all_sums[line] = total
        for k in range(1, lines):
            all_copy(k, line).start()

    def image_step(c, carry):
        forward(IMG, c)
        norms(IMG, 1, c)

        @pl.when(c == 0)
        def _():
            from_sides(TXT, CHUNKS - 1)

        own_pairs(c)

        pl.when(c == CHUNKS - 1)(line_total)
        from_sides(IMG, c)
        side_pairs(c)
        return carry

    lax.fori_loop(0, CHUNKS, image_step, 0)

    for c in range(CHUNKS):
        here = pl.ds(c * CHUNK, CHUNK)
        inverse = inv_row[TXT, 1, 0:1, here]
        along_row = row_of(txt_along[here, :]) * inverse
        wide = held[TXT, pl.ds(0, PART), columns_of(1, c)].astype(F32)
        result = (inverse * scale) * (txt_grad[:, here] - wide * (inverse * along_row))
        txt_out[:, here] = result.astype(BF16)

    for k in range(1, lines):
        all_copy(k, all_peer(k)[0]).wait_recv()
    total = all_sums[0]
    for k in range(1, lines):
        total = total + all_sums[k]
    total = total * (1.0 / (2.0 * count * SUPER * 5 * BLOCK))
    for n in range(3):
        sums_out[n] = jnp.max(total[n : n + 1, :])

    for a in range(2):
        for c in range(CHUNKS):
            x_copy(a, c).wait_send()
            for side in range(2):
                own_copy(a, side, c).wait_send()
                other_copy(a, side, c).wait_send()
    for side in range(2):
        weight_copy(side).wait_send()
    for k in range(1, 2 * LINE):
        line_copy(k, rank).wait_send()
    for k in range(1, lines):
        all_copy(k, line).wait_send()


def shards(count, vision, caption, importance, scale_exponent, similarity_shift):
    lines = count // LINE
    dma = pltpu.SemaphoreType.DMA
    hbm, vmem = pl.BlockSpec(memory_space=pl.ANY), pl.BlockSpec(memory_space=pltpu.VMEM)
    smem = pl.BlockSpec(memory_space=pltpu.SMEM)
    img_out, txt_out, sums = pl.pallas_call(
        functools.partial(kernel, count),
        out_shape=(
            pltpu.VMEM((PART, SUPER), BF16),
            pltpu.VMEM((PART, SUPER), BF16),
            jax.ShapeDtypeStruct((3,), F32),
        ),
        in_specs=[hbm, hbm, vmem, smem, smem],
        out_specs=(vmem, vmem, smem),
        scratch_shapes=[
            pltpu.VMEM((2, FULL, 3 * SUPER), BF16),
            pltpu.VMEM((3, 8, SUPER), F32),
            pltpu.VMEM((2, 3, 8, SUPER), F32),
            pltpu.VMEM((2, SUPER, 128), F32),
            pltpu.VMEM((SUPER, FULL), BF16),
            pltpu.VMEM((CHUNK, FULL), BF16),
            pltpu.VMEM((PART, SUPER), F32),
            pltpu.VMEM((SUPER, 128), F32),
            pltpu.VMEM((8, 128), F32),
            pltpu.VMEM((CHUNK, 5 * BLOCK), BF16),
            pltpu.VMEM((2 * LINE, 8, 128), F32),
            pltpu.VMEM((8, 128), F32),
            pltpu.VMEM((lines, 8, 128), F32),
            dma((2,)),
            dma((2, CHUNKS)),
            dma((2, CHUNKS)),
            dma((2, 2, CHUNKS)),
            dma((2, 2, CHUNKS)),
            dma((2, 2, CHUNKS)),
            dma((2, 2, CHUNKS)),
            dma((2,)),
            dma((2,)),
            dma((2 * LINE,)),
            dma((2 * LINE,)),
            dma((lines,)),
            dma((lines,)),
        ],
        compiler_params=pltpu.CompilerParams(
            collective_id=0, has_side_effects=True, vmem_limit_bytes=60 * 2**20
        ),
        name="band",
    )(caption.T, vision.T, importance.reshape(8, SUPER // 8), scale_exponent, similarity_shift)
    return img_out.T, txt_out.T, sums


def solution(mesh):
    in_specs = (P("blk", "tower"), P("blk", "tower"), P("blk"), P(), P())
    out_specs = (P("blk", "tower"), P("blk", "tower"), P())
    return jax.shard_map(
        functools.partial(shards, mesh.shape["blk"]),
        mesh=mesh,
        in_specs=in_specs,
        out_specs=out_specs,
        check_vma=False,
    )
```

```python
import functools
import math

import jax
import jax.numpy as jnp
from jax import lax
from jax.experimental import pallas as pl
from jax.experimental.pallas import tpu as pltpu
from jax.sharding import PartitionSpec as P

MESH = pl.DeviceIdType.MESH
F32, BF16 = jnp.float32, jnp.bfloat16
TXT, IMG = 0, 1
BLOCK = 512
SUPER = 1024
PART = 576
FULL = 1152
CHUNK = 256
CHUNKS = SUPER // CHUNK
AHEAD = 1
LINE = 8
LOG2E = math.log2(math.e)


def fold(v):
    total = v[:, :128]
    for k in range(1, v.shape[1] // 128):
        total = total + v[:, 128 * k : 128 * (k + 1)]
    return total


def row_of(partial):
    return jnp.sum(jnp.transpose(partial), axis=0, keepdims=True)


def kernel(
    count,
    txt_in,
    img_in,
    weight_in,
    exponent,
    offset,
    img_out,
    txt_out,
    sums_out,
    held,
    weights,
    inv_row,
    inv_col,
    turned_txt,
    turned_img,
    txt_grad,
    txt_along,
    tallies,
    coef,
    line_sums,
    line_out,
    all_sums,
    load_sem,
    x_send,
    x_recv,
    own_send,
    own_recv,
    other_send,
    other_recv,
    weight_send,
    weight_recv,
    line_send,
    line_recv,
    all_send,
    all_recv,
):
    sb = lax.axis_index("blk")
    tower = lax.axis_index("tower")
    away = 1 - tower
    left, right = lax.rem(sb + count - 1, count), lax.rem(sb + 1, count)
    place, line = lax.rem(sb, LINE), sb // LINE
    lines = count // LINE
    rank = place * 2 + tower
    left_end, right_end = place == 0, place == LINE - 1
    inputs = (txt_in, img_in)
    sides = ((0, left, left_end), (1, right, right_end))

    def line_peer(k):
        there = lax.rem(rank + k, 2 * LINE)
        return there, (line * LINE + there // 2, lax.rem(there, 2))

    def all_peer(k):
        there = lax.rem(line + k, lines)
        return there, (there * LINE + place, tower)

    def columns_of(slot, c):
        return pl.ds(pl.multiple_of(slot * SUPER + c * CHUNK, CHUNK), CHUNK)

    def whole(slot):
        return pl.ds(slot * SUPER, SUPER)

    loads = []
    for a in range(2):
        target = held.at[a, pl.ds(0, PART), whole(1)]
        loads.append(pltpu.make_async_copy(inputs[a], target, load_sem.at[a]))
        loads[a].start()

    barrier = pltpu.get_barrier_semaphore()

    def greet(where):
        pl.semaphore_signal(barrier, inc=1, device_id=where, device_id_type=MESH)

    for where in ((sb, away), (left, tower), (right, tower)):
        greet(where)

    @pl.when(left_end)
    def _():
        greet((left, away))

    @pl.when(right_end)
    def _():
        greet((right, away))

    def greet_line(k, carry):
        greet(line_peer(k)[1])
        return carry

    def greet_all(k, carry):
        greet(all_peer(k)[1])
        return carry

    lax.fori_loop(1, 2 * LINE, greet_line, 0)
    lax.fori_loop(1, lines, greet_all, 0)
    at_end = jnp.logical_or(left_end, right_end)
    pl.semaphore_wait(barrier, jnp.where(at_end, 4, 3) + (2 * LINE - 1) + (lines - 1))

    def x_copy(a, c):
        return pltpu.make_async_remote_copy(
            src_ref=inputs[a].at[:, pl.ds(c * CHUNK, CHUNK)],
            dst_ref=held.at[a, pl.ds(PART, PART), columns_of(1, c)],
            send_sem=x_send.at[a, c],
            recv_sem=x_recv.at[a, c],
            device_id=(sb, away),
            device_id_type=MESH,
        )

    def own_copy(a, side, c):
        n, where, _ = sides[side]
        return pltpu.make_async_remote_copy(
            src_ref=inputs[a].at[:, pl.ds(c * CHUNK, CHUNK)],
            dst_ref=held.at[a, pl.ds(0, PART), columns_of(2 - 2 * n, c)],
            send_sem=own_send.at[a, n, c],
            recv_sem=own_recv.at[a, n, c],
            device_id=(where, tower),
            device_id_type=MESH,
        )

    def other_copy(a, side, c, cross=False):
        n, where, _ = sides[side]
        here = pl.ds(c * CHUNK, CHUNK)
        return pltpu.make_async_remote_copy(
            src_ref=inputs[a].at[:, here] if cross else held.at[a, pl.ds(PART, PART), columns_of(1, c)],
            dst_ref=held.at[a, pl.ds(PART, PART), columns_of(2 - 2 * n, c)],
            send_sem=other_send.at[a, n, c],
            recv_sem=other_recv.at[a, n, c],
            device_id=(where, away if cross else tower),
            device_id_type=MESH,
        )

    def begin(a, c):
        x_copy(a, c).start()

    def begin_sides(a, c):
        for side in range(2):
            own_copy(a, side, c).start()

            @pl.when(sides[side][2])
            def _():
                other_copy(a, side, c, cross=True).start()

    def weight_copy(side):
        n, where, _ = sides[side]
        return pltpu.make_async_remote_copy(
            src_ref=weights.at[1],
            dst_ref=weights.at[2 - 2 * n],
            send_sem=weight_send.at[n],
            recv_sem=weight_recv.at[n],
            device_id=(where, tower),
            device_id_type=MESH,
        )

    def line_copy(k, source):
        there, where = line_peer(k)
        return pltpu.make_async_remote_copy(
            src_ref=tallies,
            dst_ref=line_sums.at[source],
            send_sem=line_send.at[k],
            recv_sem=line_recv.at[source],
            device_id=where,
            device_id_type=MESH,
        )

    def all_copy(k, source):
        there, where = all_peer(k)
        return pltpu.make_async_remote_copy(
            src_ref=line_out,
            dst_ref=all_sums.at[source],
            send_sem=all_send.at[k],
            recv_sem=all_recv.at[source],
            device_id=where,
            device_id_type=MESH,
        )

    for c in range(AHEAD):
        begin(TXT, c)
        begin_sides(TXT, c)
    heavy = weight_in[...].astype(F32)
    for k in range(8):
        weights[1, :, 128 * k : 128 * (k + 1)] = jnp.broadcast_to(heavy[k : k + 1], (8, 128))
    for side in range(2):
        weight_copy(side).start()

    scale = jnp.exp(jnp.full((1, 128), exponent[0], F32))[:, 0:1]
    scale2 = scale * LOG2E
    shift2 = offset[0] * LOG2E

    txt_grad[...] = jnp.zeros_like(txt_grad)
    txt_along[...] = jnp.zeros_like(txt_along)
    tallies[...] = jnp.zeros_like(tallies)
    for load in loads:
        load.wait()

    def norms(a, slot, c):
        wide = held[a, :, columns_of(slot, c)].astype(F32)
        total = jnp.sum(wide * wide, axis=0, keepdims=True)
        inverse = lax.rsqrt(total + 1e-06)
        here = pl.ds(pl.multiple_of(c * CHUNK, CHUNK), CHUNK)
        inv_row[a, slot, :, here] = jnp.broadcast_to(inverse, (8, CHUNK))
        if slot == 1:
            inv_col[a, here, :] = jnp.transpose(jnp.broadcast_to(inverse, (128, CHUNK)))

    def ahead(a, c, start):
        @pl.when(c < CHUNKS - AHEAD)
        def _():
            start(a, c + AHEAD)

        if a == TXT:

            @pl.when(c >= CHUNKS - AHEAD)
            def _():
                start(IMG, c - (CHUNKS - AHEAD))

    def forward(a, c):
        ahead(a, c, begin)
        x_copy(a, c).wait_recv()
        for side in range(2):
            pl.when(jnp.logical_not(sides[side][2]))(other_copy(a, side, c).start)
        ahead(a, c, begin_sides)

    def from_sides(a, c):
        for side in range(2):
            own_copy(a, 1 - side, c).wait_recv()
            other_copy(a, 1 - side, c).wait_recv()
            norms(a, 2 * side, c)

    def text_step(c, carry):
        forward(TXT, c)
        norms(TXT, 1, c)
        here = pl.ds(pl.multiple_of(c * CHUNK, CHUNK), CHUNK)
        turned_txt[here, :] = jnp.transpose(held[TXT, :, columns_of(1, c)])

        @pl.when(c > 0)
        def _():
            from_sides(TXT, c - 1)

        return carry

    lax.fori_loop(0, CHUNKS, text_step, 0)
    for side in range(2):
        weight_copy(1 - side).wait_recv()

    def image_product(c, j):
        first = pl.multiple_of((c // 2 + j) * BLOCK, BLOCK)
        return jnp.dot(
            turned_img[...], held[TXT, :, pl.ds(first, BLOCK)], preferred_element_type=F32
        )

    def image_coef(c, j, product, sums):
        along, bias, loss = sums
        here = pl.ds(pl.multiple_of(c * CHUNK, CHUNK), CHUNK)
        row_scale = inv_col[IMG, here, 0:1] * scale2
        first = pl.multiple_of((c // 2 + j) * BLOCK, BLOCK)
        slot, inside = first // SUPER, lax.rem(first, SUPER)
        inv_text = inv_row[TXT, slot, 0:1, pl.ds(pl.multiple_of(inside, BLOCK), BLOCK)]
        logits2 = product * inv_text * row_scale + shift2
        grown = jnp.exp2(logits2)
        more = grown + 1.0
        sig = grown / more
        loss = loss + fold(jnp.log(more[:, :CHUNK] * more[:, CHUNK:]))
        if j == 2:
            mine = lax.broadcasted_iota(jnp.int32, (CHUNK, BLOCK), 0) + lax.rem(c, 2) * CHUNK
            match = mine == lax.broadcasted_iota(jnp.int32, (CHUNK, BLOCK), 1)
            sig = jnp.where(match, sig - 1.0, sig)
            loss = loss - fold(jnp.where(match, logits2, 0.0)) * (1.0 / LOG2E)
        scaled = sig * inv_text
        along = along + fold(scaled * product)
        bias = bias + fold(sig)
        coef[:, pl.ds(j * BLOCK, BLOCK)] = scaled.astype(BF16)
        return along, bias, loss

    def image_grad(c, sums):
        along, bias, loss = sums
        here = pl.ds(pl.multiple_of(c * CHUNK, CHUNK), CHUNK)
        band = pl.ds(pl.multiple_of(c // 2 * BLOCK, BLOCK), 5 * BLOCK)
        grad = lax.dot_general(
            held[TXT, pl.ds(0, PART), band],
            coef[...],
            (((1,), (1,)), ((), ())),
            preferred_element_type=F32,
        )
        weight = weights[1, 0:1, here]
        inverse = inv_row[IMG, 1, 0:1, here]
        along_row = row_of(along) * inverse
        wide = held[IMG, pl.ds(0, PART), columns_of(1, c)].astype(F32)
        result = (weight * inverse * scale) * (grad - wide * (inverse * along_row))
        img_out[:, here] = result.astype(BF16)
        for n, value in enumerate((row_of(loss), scale * along_row, row_of(bias))):
            total = jnp.sum(weight * value, axis=1, keepdims=True)
            tallies[n : n + 1, :] += jnp.broadcast_to(total, (1, 128))

    def text_product(slot, c, block):
        rows = pl.ds(pl.multiple_of(block * BLOCK, BLOCK), BLOCK)
        return jnp.dot(
            turned_txt[rows, :], held[IMG, :, columns_of(slot, c)], preferred_element_type=F32
        )

    def text_coef(slot, c, block, product, diagonal):
        rows = pl.ds(pl.multiple_of(block * BLOCK, BLOCK), BLOCK)
        here = pl.ds(pl.multiple_of(c * CHUNK, CHUNK), CHUNK)
        inv_image = inv_row[IMG, slot, 0:1, here]
        heavy = inv_image * weights[slot, 0:1, here]
        row_scale = inv_col[TXT, rows, 0:1] * scale2
        grown = jnp.exp2(product * inv_image * row_scale + shift2)
        sig = grown / (grown + 1.0)
        if diagonal:
            mine = lax.broadcasted_iota(jnp.int32, (BLOCK, CHUNK), 0) + block * BLOCK
            other = lax.broadcasted_iota(jnp.int32, (BLOCK, CHUNK), 1) + c * CHUNK
            sig = jnp.where(mine == other, sig - 1.0, sig)
        scaled = sig * heavy
        txt_along[rows, :] += fold(scaled * product)
        return scaled.astype(BF16)

    def text_grad(slot, c, block, scaled):
        rows = pl.ds(pl.multiple_of(block * BLOCK, BLOCK), BLOCK)
        txt_grad[:, rows] += lax.dot_general(
            held[IMG, pl.ds(0, PART), columns_of(slot, c)],
            scaled,
            (((1,), (1,)), ((), ())),
            preferred_element_type=F32,
        )

    def own_pairs(c):
        turned_img[...] = jnp.transpose(held[IMG, :, columns_of(1, c)])
        zero = jnp.zeros((CHUNK, 128), F32)
        sums = (zero, zero, zero)
        product = image_product(c, 0)
        for j in range(5):
            after = image_product(c, j + 1) if j < 4 else None
            sums = image_coef(c, j, product, sums)
            product = after
        image_grad(c, sums)

        @pl.when(c == CHUNKS - 1)
        def _():
            for k in range(1, 2 * LINE):
                line_copy(k, rank).start()

        product = text_product(1, c, 0)
        after = text_product(1, c, 1)
        scaled = text_coef(1, c, 0, product, True)
        text_grad(1, c, 0, scaled)
        scaled = text_coef(1, c, 1, after, True)
        text_grad(1, c, 1, scaled)

    def side_pairs(c):
        late = c >= CHUNKS // 2
        jobs = [(0, 0), (2, 1), (jnp.where(late, 0, 2), jnp.where(late, 1, 0))]
        product = text_product(jobs[0][0], c, jobs[0][1])
        for n, (slot, block) in enumerate(jobs):
            after = text_product(jobs[n + 1][0], c, jobs[n + 1][1]) if n < 2 else None
            scaled = text_coef(slot, c, block, product, False)
            text_grad(slot, c, block, scaled)
            product = after

    def line_total():
        line_sums[rank] = tallies[...]
        for k in range(1, 2 * LINE):
            line_copy(k, line_peer(k)[0]).wait_recv()
        total = line_sums[0]
        for k in range(1, 2 * LINE):
            total = total + line_sums[k]
        line_out[...] = total
        all_sums[line] = total
        for k in range(1, lines):
            all_copy(k, line).start()

    def image_step(c, carry):
        forward(IMG, c)
        norms(IMG, 1, c)

        @pl.when(c == 0)
        def _():
            from_sides(TXT, CHUNKS - 1)

        own_pairs(c)

        pl.when(c == CHUNKS - 1)(line_total)
        from_sides(IMG, c)
        side_pairs(c)
        return carry

    lax.fori_loop(0, CHUNKS, image_step, 0)

    for c in range(CHUNKS):
        here = pl.ds(c * CHUNK, CHUNK)
        inverse = inv_row[TXT, 1, 0:1, here]
        along_row = row_of(txt_along[here, :]) * inverse
        wide = held[TXT, pl.ds(0, PART), columns_of(1, c)].astype(F32)
        result = (inverse * scale) * (txt_grad[:, here] - wide * (inverse * along_row))
        txt_out[:, here] = result.astype(BF16)

    for k in range(1, lines):
        all_copy(k, all_peer(k)[0]).wait_recv()
    total = all_sums[0]
    for k in range(1, lines):
        total = total + all_sums[k]
    total = total * (1.0 / (2.0 * count * SUPER * 5 * BLOCK))
    for n in range(3):
        sums_out[n] = jnp.max(total[n : n + 1, :])

    for a in range(2):
        for c in range(CHUNKS):
            x_copy(a, c).wait_send()
            for side in range(2):
                own_copy(a, side, c).wait_send()
                other_copy(a, side, c).wait_send()
    for side in range(2):
        weight_copy(side).wait_send()
    for k in range(1, 2 * LINE):
        line_copy(k, rank).wait_send()
    for k in range(1, lines):
        all_copy(k, line).wait_send()


def shards(count, vision, caption, importance, scale_exponent, similarity_shift):
    lines = count // LINE
    dma = pltpu.SemaphoreType.DMA
    hbm, vmem = pl.BlockSpec(memory_space=pl.ANY), pl.BlockSpec(memory_space=pltpu.VMEM)
    smem = pl.BlockSpec(memory_space=pltpu.SMEM)
    img_out, txt_out, sums = pl.pallas_call(
        functools.partial(kernel, count),
        out_shape=(
            pltpu.VMEM((PART, SUPER), BF16),
            pltpu.VMEM((PART, SUPER), BF16),
            jax.ShapeDtypeStruct((3,), F32),
        ),
        in_specs=[hbm, hbm, vmem, smem, smem],
        out_specs=(vmem, vmem, smem),
        scratch_shapes=[
            pltpu.VMEM((2, FULL, 3 * SUPER), BF16),
            pltpu.VMEM((3, 8, SUPER), F32),
            pltpu.VMEM((2, 3, 8, SUPER), F32),
            pltpu.VMEM((2, SUPER, 128), F32),
            pltpu.VMEM((SUPER, FULL), BF16),
            pltpu.VMEM((CHUNK, FULL), BF16),
            pltpu.VMEM((PART, SUPER), F32),
            pltpu.VMEM((SUPER, 128), F32),
            pltpu.VMEM((8, 128), F32),
            pltpu.VMEM((CHUNK, 5 * BLOCK), BF16),
            pltpu.VMEM((2 * LINE, 8, 128), F32),
            pltpu.VMEM((8, 128), F32),
            pltpu.VMEM((lines, 8, 128), F32),
            dma((2,)),
            dma((2, CHUNKS)),
            dma((2, CHUNKS)),
            dma((2, 2, CHUNKS)),
            dma((2, 2, CHUNKS)),
            dma((2, 2, CHUNKS)),
            dma((2, 2, CHUNKS)),
            dma((2,)),
            dma((2,)),
            dma((2 * LINE,)),
            dma((2 * LINE,)),
            dma((lines,)),
            dma((lines,)),
        ],
        compiler_params=pltpu.CompilerParams(
            collective_id=0, has_side_effects=True, vmem_limit_bytes=60 * 2**20
        ),
        name="band",
    )(caption.T, vision.T, importance.reshape(8, SUPER // 8), scale_exponent, similarity_shift)
    return img_out.T, txt_out.T, sums


def solution(mesh):
    in_specs = (P("blk", "tower"), P("blk", "tower"), P("blk"), P(), P())
    out_specs = (P("blk", "tower"), P("blk", "tower"), P())
    return jax.shard_map(
        functools.partial(shards, mesh.shape["blk"]),
        mesh=mesh,
        in_specs=in_specs,
        out_specs=out_specs,
        check_vma=False,
    )
```

```python
import functools
import math

import jax
import jax.numpy as jnp
from jax import lax
from jax.experimental import pallas as pl
from jax.experimental.pallas import tpu as pltpu
from jax.sharding import PartitionSpec as P

MESH = pl.DeviceIdType.MESH
F32, BF16 = jnp.float32, jnp.bfloat16
TXT, IMG = 0, 1
BLOCK = 512
SUPER = 1024
PART = 576
FULL = 1152
CHUNK = 256
CHUNKS = SUPER // CHUNK
AHEAD = 1
HALVES = 2
LINE = 8
LOG2E = math.log2(math.e)


def fold(v):
    total = v[:, :128]
    for k in range(1, v.shape[1] // 128):
        total = total + v[:, 128 * k : 128 * (k + 1)]
    return total


def row_of(partial):
    return jnp.sum(jnp.transpose(partial), axis=0, keepdims=True)


def kernel(
    count,
    txt_in,
    img_in,
    weight_in,
    exponent,
    offset,
    img_out,
    txt_out,
    sums_out,
    held,
    weights,
    inv_row,
    inv_col,
    turned_txt,
    turned_img,
    txt_grad,
    txt_along,
    tallies,
    coef,
    line_sums,
    line_out,
    all_sums,
    load_sem,
    x_send,
    x_recv,
    own_send,
    own_recv,
    other_send,
    other_recv,
    weight_send,
    weight_recv,
    line_send,
    line_recv,
    all_send,
    all_recv,
):
    sb = lax.axis_index("blk")
    tower = lax.axis_index("tower")
    away = 1 - tower
    left, right = lax.rem(sb + count - 1, count), lax.rem(sb + 1, count)
    place, line = lax.rem(sb, LINE), sb // LINE
    lines = count // LINE
    rank = place * 2 + tower
    left_end, right_end = place == 0, place == LINE - 1
    inputs = (txt_in, img_in)
    sides = ((0, left, left_end), (1, right, right_end))

    def line_peer(k):
        there = lax.rem(rank + k, 2 * LINE)
        return there, (line * LINE + there // 2, lax.rem(there, 2))

    def all_peer(k):
        there = lax.rem(line + k, lines)
        return there, (there * LINE + place, tower)

    def columns_of(slot, c):
        return pl.ds(pl.multiple_of(slot * SUPER + c * CHUNK, CHUNK), CHUNK)

    def whole(slot):
        return pl.ds(slot * SUPER, SUPER)

    loads = []
    for a in range(2):
        target = held.at[a, pl.ds(0, PART), whole(1)]
        loads.append(pltpu.make_async_copy(inputs[a], target, load_sem.at[a]))
        loads[a].start()

    barrier = pltpu.get_barrier_semaphore()

    def greet(where):
        pl.semaphore_signal(barrier, inc=1, device_id=where, device_id_type=MESH)

    for where in ((sb, away), (left, tower), (right, tower)):
        greet(where)

    @pl.when(left_end)
    def _():
        greet((left, away))

    @pl.when(right_end)
    def _():
        greet((right, away))

    def greet_line(k, carry):
        greet(line_peer(k)[1])
        return carry

    def greet_all(k, carry):
        greet(all_peer(k)[1])
        return carry

    lax.fori_loop(1, 2 * LINE, greet_line, 0)
    lax.fori_loop(1, lines, greet_all, 0)
    at_end = jnp.logical_or(left_end, right_end)
    pl.semaphore_wait(barrier, jnp.where(at_end, 4, 3) + (2 * LINE - 1) + (lines - 1))

    def x_copy(a, c, h):
        rows = PART // HALVES
        return pltpu.make_async_remote_copy(
            src_ref=inputs[a].at[pl.ds(h * rows, rows), pl.ds(c * CHUNK, CHUNK)],
            dst_ref=held.at[a, pl.ds(PART + h * rows, rows), columns_of(1, c)],
            send_sem=x_send.at[a, c, h],
            recv_sem=x_recv.at[a, c, h],
            device_id=(sb, away),
            device_id_type=MESH,
        )

    def own_copy(a, side, c):
        n, where, _ = sides[side]
        return pltpu.make_async_remote_copy(
            src_ref=inputs[a].at[:, pl.ds(c * CHUNK, CHUNK)],
            dst_ref=held.at[a, pl.ds(0, PART), columns_of(2 - 2 * n, c)],
            send_sem=own_send.at[a, n, c],
            recv_sem=own_recv.at[a, n, c],
            device_id=(where, tower),
            device_id_type=MESH,
        )

    def other_copy(a, side, c, cross=False):
        n, where, _ = sides[side]
        here = pl.ds(c * CHUNK, CHUNK)
        return pltpu.make_async_remote_copy(
            src_ref=inputs[a].at[:, here] if cross else held.at[a, pl.ds(PART, PART), columns_of(1, c)],
            dst_ref=held.at[a, pl.ds(PART, PART), columns_of(2 - 2 * n, c)],
            send_sem=other_send.at[a, n, c],
            recv_sem=other_recv.at[a, n, c],
            device_id=(where, away if cross else tower),
            device_id_type=MESH,
        )

    def begin(a, c):
        for h in range(HALVES):
            x_copy(a, c, h).start()

    def begin_sides(a, c):
        for side in range(2):
            own_copy(a, side, c).start()

            @pl.when(sides[side][2])
            def _():
                other_copy(a, side, c, cross=True).start()

    def weight_copy(side):
        n, where, _ = sides[side]
        return pltpu.make_async_remote_copy(
            src_ref=weights.at[1],
            dst_ref=weights.at[2 - 2 * n],
            send_sem=weight_send.at[n],
            recv_sem=weight_recv.at[n],
            device_id=(where, tower),
            device_id_type=MESH,
        )

    def line_copy(k, source):
        there, where = line_peer(k)
        return pltpu.make_async_remote_copy(
            src_ref=tallies,
            dst_ref=line_sums.at[source],
            send_sem=line_send.at[k],
            recv_sem=line_recv.at[source],
            device_id=where,
            device_id_type=MESH,
        )

    def all_copy(k, source):
        there, where = all_peer(k)
        return pltpu.make_async_remote_copy(
            src_ref=line_out,
            dst_ref=all_sums.at[source],
            send_sem=all_send.at[k],
            recv_sem=all_recv.at[source],
            device_id=where,
            device_id_type=MESH,
        )

    for c in range(AHEAD):
        begin(TXT, c)
        begin_sides(TXT, c)
    heavy = weight_in[...].astype(F32)
    for k in range(8):
        weights[1, :, 128 * k : 128 * (k + 1)] = jnp.broadcast_to(heavy[k : k + 1], (8, 128))
    for side in range(2):
        weight_copy(side).start()

    scale = jnp.exp(jnp.full((1, 128), exponent[0], F32))[:, 0:1]
    scale2 = scale * LOG2E
    shift2 = offset[0] * LOG2E

    txt_grad[...] = jnp.zeros_like(txt_grad)
    txt_along[...] = jnp.zeros_like(txt_along)
    tallies[...] = jnp.zeros_like(tallies)
    for load in loads:
        load.wait()

    def norms(a, slot, c):
        wide = held[a, :, columns_of(slot, c)].astype(F32)
        total = jnp.sum(wide * wide, axis=0, keepdims=True)
        inverse = lax.rsqrt(total + 1e-06)
        here = pl.ds(pl.multiple_of(c * CHUNK, CHUNK), CHUNK)
        inv_row[a, slot, :, here] = jnp.broadcast_to(inverse, (8, CHUNK))
        if slot == 1:
            inv_col[a, here, :] = jnp.transpose(jnp.broadcast_to(inverse, (128, CHUNK)))

    def ahead(a, c, start):
        @pl.when(c < CHUNKS - AHEAD)
        def _():
            start(a, c + AHEAD)

        if a == TXT:

            @pl.when(c >= CHUNKS - AHEAD)
            def _():
                start(IMG, c - (CHUNKS - AHEAD))

    def forward(a, c):
        ahead(a, c, begin)
        for h in range(HALVES):
            x_copy(a, c, h).wait_recv()
        for side in range(2):
            pl.when(jnp.logical_not(sides[side][2]))(other_copy(a, side, c).start)
        ahead(a, c, begin_sides)

    def from_sides(a, c):
        for side in range(2):
            own_copy(a, 1 - side, c).wait_recv()
            other_copy(a, 1 - side, c).wait_recv()
            norms(a, 2 * side, c)

    def text_step(c, carry):
        forward(TXT, c)
        norms(TXT, 1, c)
        here = pl.ds(pl.multiple_of(c * CHUNK, CHUNK), CHUNK)
        turned_txt[here, :] = jnp.transpose(held[TXT, :, columns_of(1, c)])

        @pl.when(c > 0)
        def _():
            from_sides(TXT, c - 1)

        return carry

    lax.fori_loop(0, CHUNKS, text_step, 0)
    for side in range(2):
        weight_copy(1 - side).wait_recv()

    def image_product(c, j):
        first = pl.multiple_of((c // 2 + j) * BLOCK, BLOCK)
        return jnp.dot(
            turned_img[...], held[TXT, :, pl.ds(first, BLOCK)], preferred_element_type=F32
        )

    def image_coef(c, j, product, sums):
        along, bias, loss = sums
        here = pl.ds(pl.multiple_of(c * CHUNK, CHUNK), CHUNK)
        row_scale = inv_col[IMG, here, 0:1] * scale2
        first = pl.multiple_of((c // 2 + j) * BLOCK, BLOCK)
        slot, inside = first // SUPER, lax.rem(first, SUPER)
        inv_text = inv_row[TXT, slot, 0:1, pl.ds(pl.multiple_of(inside, BLOCK), BLOCK)]
        logits2 = product * inv_text * row_scale + shift2
        grown = jnp.exp2(logits2)
        more = grown + 1.0
        sig = grown / more
        loss = loss + fold(jnp.log(more[:, :CHUNK] * more[:, CHUNK:]))
        if j == 2:
            mine = lax.broadcasted_iota(jnp.int32, (CHUNK, BLOCK), 0) + lax.rem(c, 2) * CHUNK
            match = mine == lax.broadcasted_iota(jnp.int32, (CHUNK, BLOCK), 1)
            sig = jnp.where(match, sig - 1.0, sig)
            loss = loss - fold(jnp.where(match, logits2, 0.0)) * (1.0 / LOG2E)
        scaled = sig * inv_text
        along = along + fold(scaled * product)
        bias = bias + fold(sig)
        coef[:, pl.ds(j * BLOCK, BLOCK)] = scaled.astype(BF16)
        return along, bias, loss

    def image_grad(c, sums):
        along, bias, loss = sums
        here = pl.ds(pl.multiple_of(c * CHUNK, CHUNK), CHUNK)
        band = pl.ds(pl.multiple_of(c // 2 * BLOCK, BLOCK), 5 * BLOCK)
        grad = lax.dot_general(
            held[TXT, pl.ds(0, PART), band],
            coef[...],
            (((1,), (1,)), ((), ())),
            preferred_element_type=F32,
        )
        weight = weights[1, 0:1, here]
        inverse = inv_row[IMG, 1, 0:1, here]
        along_row = row_of(along) * inverse
        wide = held[IMG, pl.ds(0, PART), columns_of(1, c)].astype(F32)
        result = (weight * inverse * scale) * (grad - wide * (inverse * along_row))
        img_out[:, here] = result.astype(BF16)
        for n, value in enumerate((row_of(loss), scale * along_row, row_of(bias))):
            total = jnp.sum(weight * value, axis=1, keepdims=True)
            tallies[n : n + 1, :] += jnp.broadcast_to(total, (1, 128))

    def text_product(slot, c, block):
        rows = pl.ds(pl.multiple_of(block * BLOCK, BLOCK), BLOCK)
        return jnp.dot(
            turned_txt[rows, :], held[IMG, :, columns_of(slot, c)], preferred_element_type=F32
        )

    def text_coef(slot, c, block, product, diagonal):
        rows = pl.ds(pl.multiple_of(block * BLOCK, BLOCK), BLOCK)
        here = pl.ds(pl.multiple_of(c * CHUNK, CHUNK), CHUNK)
        inv_image = inv_row[IMG, slot, 0:1, here]
        heavy = inv_image * weights[slot, 0:1, here]
        row_scale = inv_col[TXT, rows, 0:1] * scale2
        grown = jnp.exp2(product * inv_image * row_scale + shift2)
        sig = grown / (grown + 1.0)
        if diagonal:
            mine = lax.broadcasted_iota(jnp.int32, (BLOCK, CHUNK), 0) + block * BLOCK
            other = lax.broadcasted_iota(jnp.int32, (BLOCK, CHUNK), 1) + c * CHUNK
            sig = jnp.where(mine == other, sig - 1.0, sig)
        scaled = sig * heavy
        txt_along[rows, :] += fold(scaled * product)
        return scaled.astype(BF16)

    def text_grad(slot, c, block, scaled):
        rows = pl.ds(pl.multiple_of(block * BLOCK, BLOCK), BLOCK)
        txt_grad[:, rows] += lax.dot_general(
            held[IMG, pl.ds(0, PART), columns_of(slot, c)],
            scaled,
            (((1,), (1,)), ((), ())),
            preferred_element_type=F32,
        )

    def own_pairs(c):
        turned_img[...] = jnp.transpose(held[IMG, :, columns_of(1, c)])
        zero = jnp.zeros((CHUNK, 128), F32)
        sums = (zero, zero, zero)
        product = image_product(c, 0)
        for j in range(5):
            after = image_product(c, j + 1) if j < 4 else None
            sums = image_coef(c, j, product, sums)
            product = after
        image_grad(c, sums)

        @pl.when(c == CHUNKS - 1)
        def _():
            for k in range(1, 2 * LINE):
                line_copy(k, rank).start()

        product = text_product(1, c, 0)
        after = text_product(1, c, 1)
        scaled = text_coef(1, c, 0, product, True)
        text_grad(1, c, 0, scaled)
        scaled = text_coef(1, c, 1, after, True)
        text_grad(1, c, 1, scaled)

    def side_pairs(c):
        late = c >= CHUNKS // 2
        jobs = [(0, 0), (2, 1), (jnp.where(late, 0, 2), jnp.where(late, 1, 0))]
        product = text_product(jobs[0][0], c, jobs[0][1])
        for n, (slot, block) in enumerate(jobs):
            after = text_product(jobs[n + 1][0], c, jobs[n + 1][1]) if n < 2 else None
            scaled = text_coef(slot, c, block, product, False)
            text_grad(slot, c, block, scaled)
            product = after

    def line_total():
        line_sums[rank] = tallies[...]
        for k in range(1, 2 * LINE):
            line_copy(k, line_peer(k)[0]).wait_recv()
        total = line_sums[0]
        for k in range(1, 2 * LINE):
            total = total + line_sums[k]
        line_out[...] = total
        all_sums[line] = total
        for k in range(1, lines):
            all_copy(k, line).start()

    def image_step(c, carry):
        forward(IMG, c)
        norms(IMG, 1, c)

        @pl.when(c == 0)
        def _():
            from_sides(TXT, CHUNKS - 1)

        own_pairs(c)

        pl.when(c == CHUNKS - 1)(line_total)
        from_sides(IMG, c)
        side_pairs(c)
        return carry

    lax.fori_loop(0, CHUNKS, image_step, 0)

    for c in range(CHUNKS):
        here = pl.ds(c * CHUNK, CHUNK)
        inverse = inv_row[TXT, 1, 0:1, here]
        along_row = row_of(txt_along[here, :]) * inverse
        wide = held[TXT, pl.ds(0, PART), columns_of(1, c)].astype(F32)
        result = (inverse * scale) * (txt_grad[:, here] - wide * (inverse * along_row))
        txt_out[:, here] = result.astype(BF16)

    for k in range(1, lines):
        all_copy(k, all_peer(k)[0]).wait_recv()
    total = all_sums[0]
    for k in range(1, lines):
        total = total + all_sums[k]
    total = total * (1.0 / (2.0 * count * SUPER * 5 * BLOCK))
    for n in range(3):
        sums_out[n] = jnp.max(total[n : n + 1, :])

    for a in range(2):
        for c in range(CHUNKS):
            for h in range(HALVES):
                x_copy(a, c, h).wait_send()
            for side in range(2):
                own_copy(a, side, c).wait_send()
                other_copy(a, side, c).wait_send()
    for side in range(2):
        weight_copy(side).wait_send()
    for k in range(1, 2 * LINE):
        line_copy(k, rank).wait_send()
    for k in range(1, lines):
        all_copy(k, line).wait_send()


def shards(count, vision, caption, importance, scale_exponent, similarity_shift):
    lines = count // LINE
    dma = pltpu.SemaphoreType.DMA
    hbm, vmem = pl.BlockSpec(memory_space=pl.ANY), pl.BlockSpec(memory_space=pltpu.VMEM)
    smem = pl.BlockSpec(memory_space=pltpu.SMEM)
    img_out, txt_out, sums = pl.pallas_call(
        functools.partial(kernel, count),
        out_shape=(
            pltpu.VMEM((PART, SUPER), BF16),
            pltpu.VMEM((PART, SUPER), BF16),
            jax.ShapeDtypeStruct((3,), F32),
        ),
        in_specs=[hbm, hbm, vmem, smem, smem],
        out_specs=(vmem, vmem, smem),
        scratch_shapes=[
            pltpu.VMEM((2, FULL, 3 * SUPER), BF16),
            pltpu.VMEM((3, 8, SUPER), F32),
            pltpu.VMEM((2, 3, 8, SUPER), F32),
            pltpu.VMEM((2, SUPER, 128), F32),
            pltpu.VMEM((SUPER, FULL), BF16),
            pltpu.VMEM((CHUNK, FULL), BF16),
            pltpu.VMEM((PART, SUPER), F32),
            pltpu.VMEM((SUPER, 128), F32),
            pltpu.VMEM((8, 128), F32),
            pltpu.VMEM((CHUNK, 5 * BLOCK), BF16),
            pltpu.VMEM((2 * LINE, 8, 128), F32),
            pltpu.VMEM((8, 128), F32),
            pltpu.VMEM((lines, 8, 128), F32),
            dma((2,)),
            dma((2, CHUNKS, HALVES)),
            dma((2, CHUNKS, HALVES)),
            dma((2, 2, CHUNKS)),
            dma((2, 2, CHUNKS)),
            dma((2, 2, CHUNKS)),
            dma((2, 2, CHUNKS)),
            dma((2,)),
            dma((2,)),
            dma((2 * LINE,)),
            dma((2 * LINE,)),
            dma((lines,)),
            dma((lines,)),
        ],
        compiler_params=pltpu.CompilerParams(
            collective_id=0, has_side_effects=True, vmem_limit_bytes=60 * 2**20
        ),
        name="band",
    )(caption.T, vision.T, importance.reshape(8, SUPER // 8), scale_exponent, similarity_shift)
    return img_out.T, txt_out.T, sums


def solution(mesh):
    in_specs = (P("blk", "tower"), P("blk", "tower"), P("blk"), P(), P())
    out_specs = (P("blk", "tower"), P("blk", "tower"), P())
    return jax.shard_map(
        functools.partial(shards, mesh.shape["blk"]),
        mesh=mesh,
        in_specs=in_specs,
        out_specs=out_specs,
        check_vma=False,
    )
```
